512 devices in a mesh: ctx: 16 (over x, y_hi, core), exp: 32 (over z, y_lo).
Axes of the slice: x: 4, y: 8 (y_hi: 2, y_lo: 4; y = y_hi * 4 + y_lo), z: 8, core: 2. Of those that a mesh axis runs over, the one named last changes fastest.
Arguments:
- queries: bfloat16 [32, 2048, 2048], P('exp', 'ctx'), may hold values from -64 to 64
- key_rows: bfloat16 [32, 2048, 256], P('exp', 'ctx'), may hold values from -6 to 6
- values: bfloat16 [32, 2048, 256], P('exp', 'ctx'), may hold values from -6 to 6
- residual: bfloat16 [32, 2048, 2048], P('exp', 'ctx'), may hold values from -6 to 6
- seg_lengths: int32 [32, 32], P('exp'), may hold values from 1 to 512, 2048 in all within a row
- seg_parent: int32 [32, 32], P('exp'), may hold values from 0 to 30, as said below
- ln_gain: float32 [2048], replicated, may hold values from 0.25 to 1.75
- w_gate: bfloat16 [32, 2048, 384], P('exp', 'ctx'), may hold values from -0.125 to 0.125
- w_up: bfloat16 [32, 2048, 384], P('exp', 'ctx'), may hold values from -0.125 to 0.125
- w_down: bfloat16 [32, 384, 2048], P('exp', None, 'ctx'), may hold values from -0.3125 to 0.3125
- expert_ids: int32 [32, 2048, 8], P('exp', 'ctx'), may hold values from 0 to 127, all different within a row; in each aligned block of 128 rows (0 to 127, 128 to 255, ..., all dimensions but the last counted through in order) at most 10 rows name the same one
- gate_weights: float32 [32, 2048, 8], P('exp', 'ctx'), may hold values from 0.2 to 1
- cotangent: bfloat16 [32, 2048, 2048], P('exp', 'ctx'), may hold values from -6 to 6
Outputs:
- mixed_out: bfloat16 [32, 2048, 2048], P('exp', 'ctx')
- stream_grad: float32 [32, 2048, 2048], P('exp', 'ctx')
The draws below stay inside these ranges and needn't reach their ends.
Inputs may be any that keep to these rules, and one draw needn't show every extreme that they name: `expert_ids`: in each aligned block of 128 rows (the rows of one device) no id is named by more than 10 rows. seg_parent[b, 0] = 0, and seg_parent[b, s] < s for every segment s >= 1. `seg_lengths`: each slab's lengths sum to 2048.
All inputs are finite; a program needn't handle non-finite values.
Results may differ from the reference program's by a relative error of at most 0.0095.
Values may be sent and summed in bfloat16 or wider, within the bound.
No kernel may reach another device: no remote copies, remote signals or barrier semaphores. Data moves between devices by JAX's collectives and lax.ppermute only.
A program may use at most 64 MiB of HBM per device.

```python
import math
import jax
import jax.numpy as jnp
import numpy as np
from jax import lax

D = 2048
HEADS = 16
KV_HEADS = 2
HEAD_DIM = 128
FF = 384
ROUTED = 128
TOPK = 8
TOK_DEV = 128
SLABS = 32
SLAB_LEN = 2048
SEGS = 32
EXPERTS = 32
CAP = 10
N_CTX = 16
N_EXP = 32


def draw_key_rows(key, part):
    key = jax.random.fold_in(key, 3)
    full_shape = (SLABS, SLAB_LEN, KV_HEADS * HEAD_DIM)
    return jnp.clip(jax.random.normal(key, full_shape, jnp.float32), -6.0, 6.0).astype(jnp.bfloat16)


def draw_queries(key, part):
    key = jax.random.fold_in(key, 5)
    full_shape = (SLABS, SLAB_LEN, HEADS * HEAD_DIM)
    return jnp.clip(jax.random.normal(key, full_shape, jnp.float32), -6.0, 6.0).astype(jnp.bfloat16)


def draw_seg_parent(key, part):
    key = jax.random.fold_in(key, 7)
    segment = jnp.arange(SEGS)
    upper = jnp.broadcast_to(jnp.maximum(segment, 1), (SLABS, SEGS))
    parent = jax.random.randint(key, (SLABS, SEGS), 0, upper)
    parent = jnp.where(segment[None, :] == SEGS - 1, SEGS - 2, parent)
    return jnp.where(segment[None, :] == 0, 0, parent).astype(jnp.int32)


def levels(rng, extent, pieces, smallest, top_value):
    def one(dim, shards_of):
        steps = jax.random.uniform(jax.random.fold_in(jax.random.fold_in(rng, 6), dim), (shards_of,), jnp.float32, smallest / len(pieces), top_value / len(pieces))
        return jnp.repeat(jnp.exp(steps), extent[dim] // shards_of).reshape((-1,) + (1,) * (len(extent) - dim - 1))

    factor_of = one(*pieces[0])
    for cut in pieces[1:]:
        factor_of = factor_of * one(*cut)
    return factor_of


def profile(number_of, total, reach, lean):
    portions = [(1 << 20) // math.isqrt(standing ** lean) + 1 for standing in range(2, number_of + 1)]
    surplus, holding = total - reach - (number_of - 1), [1] * (number_of - 1)
    while surplus > 0:
        candidates = [i for i in range(number_of - 1) if holding[i] < reach]
        mass, left = sum([portions[i] for i in candidates]), surplus
        for i in candidates:
            more = min(reach - holding[i], max(1, left * portions[i] // mass), surplus)
            holding[i] = holding[i] + more
            surplus = surplus - more
    return np.array([reach] + holding)


def uneven(key, count, total, most, slope):
    if count == 2:
        one = jax.random.randint(key, (), max(1, total - most), min(most, total - 1) + 1)
        return jnp.stack([one, total - one])
    sizes = jnp.asarray(profile(count, total, most, slope), jnp.int32)
    couples = (count - 1) // 2
    source_of, receiver = sizes[1:1 + 2 * couples:2], sizes[2:2 + 2 * couples:2]
    margin = jnp.minimum(source_of - 1, most - receiver)
    shifted = jax.random.randint(jax.random.fold_in(key, 1), (couples,), 0, 1 << 20) % (margin + 1)
    sizes = sizes.at[1:1 + 2 * couples:2].set(source_of - shifted).at[2:2 + 2 * couples:2].set(receiver + shifted)
    return sizes[jax.random.permutation(jax.random.fold_in(key, 2), count)]


def deal_out(own_key, own, number, rows, count, top, most, skew):
    sequence = jax.random.permutation(own_key, count)
    heavy_load, usual = portions_of(count, rows * top, most, skew, True), portions_of(count, rows * top, most, skew, False)
    places = jnp.arange(count)

    def named(tallies, rotation):
        used = int((tallies > 0).sum())
        fixed = max(1, used // 4)
        shifted = fixed + (places - fixed + rotation * (used - fixed)) % max(1, count - fixed)
        return jnp.zeros((count,), jnp.int32).at[sequence[jnp.where(places < fixed, places, shifted)]].set(jnp.asarray(tallies, jnp.int32))

    tallies = jnp.where(number % 4 == 0, named(heavy_load, number // 4), named(usual, number - number // 4 - 1))
    mixed = jax.random.permutation(jax.random.fold_in(own, 3), count)
    giver, sink = mixed[0:count // 2 * 2:2], mixed[1:count // 2 * 2:2]
    room = jnp.minimum(tallies[giver] - 1, most - tallies[sink]) // 2
    room = jnp.where((giver == sequence[0]) | (sink == sequence[0]) | (tallies[sink] == 0), 0, jnp.maximum(room, 0))
    shifted = jax.random.randint(jax.random.fold_in(own, 4), (count // 2,), 0, 1 << 20) % (room + 1)
    tallies = tallies.at[giver].add(-shifted).at[sink].add(shifted)
    members = jnp.searchsorted(jnp.cumsum(tallies), jnp.arange(rows * top), side="right").astype(jnp.int32)
    listing = members.reshape(top, rows).T
    listing = listing[jax.random.permutation(jax.random.fold_in(own, 1), rows)]
    rotation = jax.random.randint(jax.random.fold_in(own, 2), (rows, 1), 0, top)
    return jnp.take_along_axis(listing, (jnp.arange(top)[None, :] + rotation) % top, axis=1)


def portions_of(count, total, reach, slope, full):
    portions = [(1 << 20) // math.isqrt(grade ** slope) + 1 for grade in range(1, count + 1)]
    largest = reach if full else min(reach, max(-(-total // count), total * portions[0] // sum(portions)))
    least = 1 if total - largest >= count - 1 else 0
    given, surplus = [largest] + [least] * (count - 1), total - largest - least * (count - 1)
    while surplus > 0:
        candidates = [i for i in range(1, count) if given[i] < largest] or [i for i in range(1, count) if given[i] < reach]
        pool, budget = sum([portions[i] for i in candidates]), surplus
        for i in candidates:
            more = min(reach - given[i], max(1, budget * portions[i] // pool), surplus)
            given[i] = given[i] + more
            surplus = surplus - more
    return np.array(given)


def normal_values(rng, extent, scale, limit, split=(), held_as=jnp.bfloat16):
    values = jax.random.normal(rng, extent, jnp.float32) * scale
    if len(split) > 0:
        values = levels(rng, extent, split, -0.22, 0.18) * values
    return jnp.clip(values, min=-limit, max=limit).astype(held_as)


def setup_inputs(seed: int = 0) -> dict:
    seeds = jax.random.split(jax.random.key(seed), 14)
    queries = draw_queries(jax.random.fold_in(seeds[13], 71), 0)
    key_rows = draw_key_rows(jax.random.fold_in(seeds[13], 71), 0)
    values = normal_values(seeds[2], (SLABS, SLAB_LEN, KV_HEADS * HEAD_DIM), 1.0, 6.0, ((0, 32), (1, 16)))
    residual = normal_values(seeds[3], (SLABS, SLAB_LEN, D), 1.0, 6.0, ((0, 32), (1, 16)))
    seg_lengths = jax.vmap(lambda own: uneven(own, SEGS, SLAB_LEN, SLAB_LEN // 4, 2))(jax.random.split(seeds[4], SLABS)).reshape((SLABS, SEGS)).astype(jnp.int32)
    seg_parent = draw_seg_parent(jax.random.fold_in(seeds[13], 71), 0)
    ln_gain = jnp.clip(1.0 + 0.15 * jax.random.normal(seeds[6], (D,), jnp.float32), 0.25, 1.75)
    w_gate = normal_values(seeds[7], (EXPERTS, D, FF), D ** -0.5, 0.125, ((0, 32), (1, 16)))
    w_up = normal_values(seeds[8], (EXPERTS, D, FF), D ** -0.5, 0.125, ((0, 32), (1, 16)))
    w_down = normal_values(seeds[9], (EXPERTS, FF, D), FF ** -0.5, 0.3125, ((0, 32), (2, 16)))
    expert_ids_keys = jax.random.split(jax.random.fold_in(seeds[10], 1), SLABS * SLAB_LEN // TOK_DEV)
    expert_ids_turns = jax.random.permutation(jax.random.fold_in(seeds[10], 3), SLABS * SLAB_LEN // TOK_DEV)
    expert_ids = jax.vmap(lambda own, number: deal_out(jax.random.fold_in(seeds[10], 2), own, number, TOK_DEV, ROUTED, TOPK, CAP, 1))(expert_ids_keys, expert_ids_turns).reshape((SLABS, SLAB_LEN, TOPK))
    gate_weights = jnp.clip(0.2 + 0.8 * jax.random.uniform(seeds[11], (SLABS, SLAB_LEN, TOPK), jnp.float32) ** levels(seeds[11], (SLABS, SLAB_LEN, TOPK), ((0, 32), (1, 16)), -0.2, 0.2), 0.2, 1.0)
    cotangent = normal_values(seeds[12], (SLABS, SLAB_LEN, D), 1.0, 6.0, ((0, 32), (1, 16)))
    return {"queries": queries, "key_rows": key_rows, "values": values, "residual": residual, "seg_lengths": seg_lengths, "seg_parent": seg_parent, "ln_gain": ln_gain, "w_gate": w_gate, "w_up": w_up, "w_down": w_down, "expert_ids": expert_ids, "gate_weights": gate_weights, "cotangent": cotangent}


def ancestry(parent):
    seg_count = parent.shape[0]
    index = jnp.arange(seg_count, dtype=jnp.int32)
    linked = (parent[:, None] == index[None, :]) | (index[:, None] == index[None, :])
    reached = linked.astype(jnp.float32)
    for sweep in range(max(1, (seg_count - 1).bit_length())):
        reached = jnp.minimum(jnp.dot(reached, reached, precision=lax.Precision.HIGHEST), 1.0)
    return reached

def segment_onehot(position, lengths):
    starts = jnp.cumsum(lengths) - lengths
    finish = starts + lengths
    inside = (position[:, None] >= starts[None, :]) & (position[:, None] < finish[None, :])
    return inside.astype(jnp.float32)

def slab_attention(inputs):
    query_slab, key_slab, value_slab, lengths, parent = inputs
    row_count = query_slab.shape[0]
    group_size = HEADS // KV_HEADS
    reached = ancestry(parent)
    position = jnp.arange(row_count, dtype=jnp.int32)
    member = segment_onehot(position, lengths)
    linked = jnp.dot(jnp.dot(member, reached, precision=lax.Precision.HIGHEST), member.T, precision=lax.Precision.HIGHEST)
    visible = (linked > 0.5) & (position[None, :] <= position[:, None])
    query_heads = query_slab.reshape(row_count, KV_HEADS, group_size, HEAD_DIM).astype(jnp.float32)
    key_heads = key_slab.reshape(row_count, KV_HEADS, HEAD_DIM).astype(jnp.float32)
    value_heads = value_slab.reshape(row_count, KV_HEADS, HEAD_DIM).astype(jnp.float32)
    scores = jnp.einsum('tkgd,skd->kgts', query_heads, key_heads) * HEAD_DIM ** (-0.5)
    masked = jnp.where(visible[None, None], scores, -jnp.inf)
    row_max = lax.optimization_barrier(jnp.max(masked, -1, keepdims=True))
    probs = jnp.where(visible[None, None], jnp.exp(scores - row_max), 0.0)
    denom = lax.optimization_barrier(jnp.sum(probs, -1))
    probs_low = probs.astype(jnp.bfloat16).astype(jnp.float32)
    weighted = jnp.einsum('kgts,skd->kgtd', probs_low, value_heads) / denom[..., None]
    return jnp.transpose(weighted, (2, 0, 1, 3)).reshape(row_count, HEADS * HEAD_DIM).astype(jnp.bfloat16)

def expert_pass(inputs):
    rows_in, rows_grad, weight_gate, weight_up, weight_down = inputs
    gate_proj = jnp.dot(rows_in, weight_gate, preferred_element_type=jnp.float32)
    up_proj = jnp.dot(rows_in, weight_up, preferred_element_type=jnp.float32)
    sigmoid_gate = jax.nn.sigmoid(gate_proj)
    activated = (gate_proj * sigmoid_gate * up_proj).astype(jnp.bfloat16)
    expert_out = jnp.dot(activated, weight_down, preferred_element_type=jnp.float32).astype(jnp.bfloat16)
    back_grad = jnp.dot(rows_grad, weight_down.T, preferred_element_type=jnp.float32)
    d_gate = (back_grad * up_proj * sigmoid_gate * (1.0 + gate_proj * (1.0 - sigmoid_gate))).astype(jnp.bfloat16)
    d_up = (back_grad * gate_proj * sigmoid_gate).astype(jnp.bfloat16)
    expert_grad = (jnp.dot(d_gate, weight_gate.T, preferred_element_type=jnp.float32) + jnp.dot(d_up, weight_up.T, preferred_element_type=jnp.float32)).astype(jnp.bfloat16)
    return (expert_out, expert_grad)

def reference(queries, key_rows, values, residual, seg_lengths, seg_parent, ln_gain, w_gate, w_up, w_down, expert_ids, gate_weights, cotangent):
    attended = lax.map(slab_attention, (queries, key_rows, values, seg_lengths, seg_parent))
    stream = (residual.astype(jnp.float32) + attended.astype(jnp.float32)).reshape(-1, D)
    inv_rms = lax.rsqrt(lax.optimization_barrier(jnp.mean(stream * stream, -1, keepdims=True)) + 1e-06)
    normed = (stream * inv_rms * ln_gain).astype(jnp.bfloat16)
    grad_rows = cotangent.reshape(-1, D)
    token_count = stream.shape[0]
    route_ids = expert_ids.reshape(-1)
    route_count = route_ids.shape[0]
    room = N_CTX * N_EXP * CAP
    in_window = route_ids < N_EXP
    onehot = (route_ids[:, None] == jnp.arange(N_EXP, dtype=jnp.int32)[None, :]).astype(jnp.int32)
    earlier = lax.optimization_barrier(jnp.sum((jnp.cumsum(onehot, 0) - onehot) * onehot, 1))
    slot_index = jnp.where(in_window, route_ids * room + earlier, N_EXP * room).astype(jnp.int32)
    token_index = (jnp.arange(route_count, dtype=jnp.int32) // TOPK).astype(jnp.int32)
    source = jnp.zeros((N_EXP * room,), jnp.int32).at[slot_index].set(token_index, mode='drop')
    filled = jnp.zeros((N_EXP * room,), jnp.bool_).at[slot_index].set(True, mode='drop')
    rows_in = jnp.where(filled[:, None], normed[source], 0).reshape(N_EXP, room, D)
    rows_grad = jnp.where(filled[:, None], grad_rows[source], 0).reshape(N_EXP, room, D)
    out_rows, grad_back = lax.map(expert_pass, (rows_in, rows_grad, w_gate, w_up, w_down))
    out_flat = out_rows.reshape(-1, D)
    grad_flat = grad_back.reshape(-1, D)
    take = jnp.minimum(slot_index, N_EXP * room - 1).reshape(token_count, TOPK)
    factor = jnp.where(in_window, gate_weights.reshape(-1), 0.0).reshape(token_count, TOPK)
    moe = jnp.zeros((token_count, D), jnp.float32)
    grad_normed = jnp.zeros((token_count, D), jnp.float32)
    for chosen in range(TOPK):
        moe = moe + factor[:, chosen, None] * out_flat[take[:, chosen]].astype(jnp.float32)
        grad_normed = grad_normed + factor[:, chosen, None] * grad_flat[take[:, chosen]].astype(jnp.float32)
    mixed_out = (stream + moe).astype(jnp.bfloat16)
    gain_grad = ln_gain * grad_normed
    inner = lax.optimization_barrier(jnp.mean(stream * gain_grad, -1, keepdims=True))
    stream_grad = grad_rows.astype(jnp.float32) + inv_rms * gain_grad - stream * inv_rms ** 3 * inner
    return (mixed_out.reshape(SLABS, SLAB_LEN, D), stream_grad.reshape(SLABS, SLAB_LEN, D))
```

```python
import functools
import math

import jax
import jax.numpy as jnp
from jax import lax
from jax.experimental import pallas as pl
from jax.experimental.pallas import tpu as pltpu
from jax.sharding import PartitionSpec as P

HEAD_DIM = 128
TOPK = 8
CAP = 10
BLOCK = 8
NO_SLOT = 512.0
HIDDEN = -1e30
F32 = jnp.float32
BF16 = jnp.bfloat16
NT = (((1,), (1,)), ((), ()))


def iota(shape, dim):
    return lax.broadcasted_iota(jnp.int32, shape, dim)


def dot(a, b):
    return jnp.dot(a, b, preferred_element_type=F32)


def dot_nt(a, b):
    return lax.dot_general(a, b, NT, preferred_element_type=F32)


def call(body, outs, scratch=(), flops=0, moved=0):
    return pl.pallas_call(
        body,
        out_shape=outs,
        scratch_shapes=list(scratch),
        compiler_params=pltpu.CompilerParams(vmem_limit_bytes=48 << 20),
        cost_estimate=pl.CostEstimate(flops=flops, bytes_accessed=moved, transcendentals=0),
    )


def slot_keys(ids_t, groups):
    tokens = ids_t.shape[1]
    group = iota((groups, tokens), 0)
    named = jnp.zeros((groups, tokens), F32)
    for route in range(ids_t.shape[0]):
        named = named + jnp.where(ids_t[route : route + 1, :] == group, 1.0, 0.0)
    before = (iota((tokens, tokens), 0) < iota((tokens, tokens), 1)).astype(F32)
    rank = dot(named.astype(BF16), before.astype(BF16))
    key = jnp.where(named > 0.5, rank, NO_SLOT).astype(BF16)
    rows = groups * BLOCK
    spread = (iota((rows, groups), 0) // BLOCK == iota((rows, groups), 1)).astype(F32)
    return dot(spread.astype(BF16), key)


def dispatch(rows, keys, out_ref):
    place = iota(keys.shape, 0)
    width = rows.shape[1]
    part = width // 4
    pick = jnp.where(keys == (place % BLOCK).astype(F32), 1.0, 0.0).astype(BF16)
    out_ref[:, :width] = dot(pick, rows).astype(BF16)
    late = keys == (BLOCK + (place % BLOCK) // 4).astype(F32)
    tail = jnp.zeros((keys.shape[0], part), F32)
    for k in range(4):
        pick = jnp.where(late & (place % 4 == k), 1.0, 0.0).astype(BF16)
        tail = tail + dot(pick, rows[:, k * part : (k + 1) * part])
    out_ref[:, width:] = tail.astype(BF16)


def pack_body(key_ref, value_ref, gate_ref, up_ref, down_ref, kv_ref, w_ref):
    kv_ref[:, :256] = key_ref[...]
    kv_ref[:, 256:] = value_ref[...]
    w_ref[:, :384] = gate_ref[...]
    w_ref[:, 384:768] = up_ref[...]
    w_ref[:, 768:] = down_ref[...].T


def prepare_body(groups, me_ref, cot_ref, ids_t_ref, len_row_ref, len_col_ref, parent_ref, bias_ref, send_ref):
    segs = len_row_ref.shape[1]
    rows = cot_ref.shape[0]
    low, high = iota((segs, segs), 0), iota((segs, segs), 1)
    start_col = jnp.sum(jnp.where(high < low, len_row_ref[...], 0).astype(F32), 1, keepdims=True)
    start_row = jnp.sum(jnp.where(low < high, len_col_ref[...], 0).astype(F32), 0, keepdims=True)
    finish_col = start_col + len_col_ref[...].astype(F32)
    finish_row = start_row + len_row_ref[...].astype(F32)
    reached = jnp.where((parent_ref[...] == high) | (low == high), 1.0, 0.0)
    for sweep in range(max(1, (segs - 1).bit_length())):
        low_bits = reached.astype(BF16)
        reached = jnp.minimum(dot(low_bits, low_bits), 1.0)
    me = me_ref[0]
    query_pos = (me * rows + iota((rows, 1), 0)).astype(F32)
    member = jnp.where((query_pos >= start_row) & (query_pos < finish_row), 1.0, 0.0)
    query_reach = dot(member.astype(BF16), reached.astype(BF16)).astype(BF16)
    x, y, core = me // 4, (me // 2) % 2, me % 2
    blocks = bias_ref.shape[1] // rows
    for n in range(blocks):
        half, inner = n // (blocks // 2), n % (blocks // 2)
        other = ((x + 4 - inner // 2) % 4) * 4 + (y + inner) % 2 * 2 + (core + half) % 2
        key_pos = (other * rows + iota((1, rows), 1)).astype(F32)
        holds = jnp.where((key_pos >= start_col) & (key_pos < finish_col), 1.0, 0.0)
        linked = dot(query_reach, holds.astype(BF16))
        visible = (linked > 0.5) & (key_pos <= query_pos)
        bias_ref[:, n * rows : (n + 1) * rows] = jnp.where(visible, 0.0, HIDDEN)
    dispatch(cot_ref[...], slot_keys(ids_t_ref[...], groups), send_ref)


def attend_body(
    groups,
    q_ref,
    own_ref,
    pair_ref,
    near_ref,
    far_ref,
    last_ref,
    core_ref,
    bias_ref,
    residual_ref,
    gain_ref,
    ids_t_ref,
    stream_ref,
    send_ref,
    kv_ref,
):
    first = 0
    for piece in (own_ref, pair_ref, near_ref, far_ref, last_ref, core_ref):
        kv_ref[first : first + piece.shape[0], :] = piece[...]
        first += piece.shape[0]
    kv_heads = kv_ref.shape[1] // (2 * HEAD_DIM)
    per_kv = q_ref.shape[1] // HEAD_DIM // kv_heads
    factor = HEAD_DIM**-0.5 * math.log2(math.e)
    for g in range(kv_heads):

        def head(i, carry):
            columns = pl.ds(pl.multiple_of((g * per_kv + i) * HEAD_DIM, HEAD_DIM), HEAD_DIM)
            keys = kv_ref[:, g * HEAD_DIM : (g + 1) * HEAD_DIM]
            vals = kv_ref[:, (kv_heads + g) * HEAD_DIM : (kv_heads + g + 1) * HEAD_DIM]
            scores = dot_nt(q_ref[:, columns], keys) + bias_ref[...]
            top = jnp.max(scores, -1, keepdims=True)
            probs = jnp.exp2((scores - top) * factor)
            denom = jnp.sum(probs, -1, keepdims=True)
            attended = (dot(probs.astype(BF16), vals) / denom).astype(BF16)
            stream_ref[:, columns] = residual_ref[:, columns].astype(F32) + attended.astype(F32)
            return carry

        lax.fori_loop(0, per_kv, head, 0)
    stream = stream_ref[...]
    scale_back = lax.rsqrt(jnp.mean(stream * stream, -1, keepdims=True) + 1e-06)
    normed = (stream * scale_back * gain_ref[...]).astype(BF16)
    dispatch(normed, slot_keys(ids_t_ref[...], groups), send_ref)


def expert_body(rows_ref, grads_ref, w_ref, out_ref, x_ref, g_ref):
    width = w_ref.shape[0]
    hidden = w_ref.shape[1] // 3
    main = rows_ref.shape[0]
    part = width // 4
    tails = main // 4

    def unpack(source, target):
        target[:main, :] = source[:, :width]
        tail = source[:, width:]
        at = iota((tails, main), 1) - 4 * iota((tails, main), 0)
        for k in range(4):
            pick = jnp.where(at == k, 1.0, 0.0).astype(BF16)
            target[main:, k * part : (k + 1) * part] = dot(pick, tail).astype(BF16)

    def pack(rows, first):
        out_ref[:, first : first + width] = rows[:main, :]
        at = iota((main, tails), 0) - 4 * iota((main, tails), 1)
        tail = jnp.zeros((main, part), F32)
        for k in range(4):
            pick = jnp.where(at == k, 1.0, 0.0).astype(BF16)
            tail = tail + dot(pick, rows[main:, k * part : (k + 1) * part])
        out_ref[:, first + width : first + width + part] = tail.astype(BF16)

    unpack(rows_ref, x_ref)
    unpack(grads_ref, g_ref)
    both = dot(x_ref[...], w_ref[:, : 2 * hidden])
    gate, up = both[:, :hidden], both[:, hidden:]
    sig = jax.nn.sigmoid(gate)
    silu = gate * sig
    activated = (silu * up).astype(BF16)
    pack(dot_nt(activated, w_ref[:, 2 * hidden :]).astype(BF16), 0)
    back = dot(g_ref[...], w_ref[:, 2 * hidden :])
    d_gate = (back * up * sig * (1.0 + gate * (1.0 - sig))).astype(BF16)
    d_up = (back * silu).astype(BF16)
    grad = dot_nt(d_gate, w_ref[:, :hidden]) + dot_nt(d_up, w_ref[:, hidden : 2 * hidden])
    pack(grad.astype(BF16), width + part)


def combine_body(groups, back_ref, stream_ref, cot_ref, gain_ref, ids_ref, weight_ref, mixed_ref, grad_ref, moe_ref, sum_ref):
    tokens, width = stream_ref.shape
    part = width // 4
    rows = groups * BLOCK
    group = iota((tokens, groups), 1)
    named = jnp.zeros((tokens, groups), F32)
    factor = jnp.zeros((tokens, groups), F32)
    for route in range(ids_ref.shape[1]):
        hit = ids_ref[:, route : route + 1] == group
        named = named + jnp.where(hit, 1.0, 0.0)
        factor = factor + jnp.where(hit, weight_ref[:, route : route + 1], 0.0)
    before = jnp.where(iota((tokens, tokens), 1) < iota((tokens, tokens), 0), 1.0, 0.0)
    rank = dot(before.astype(BF16), named.astype(BF16))
    key = jnp.where(named > 0.5, rank, NO_SLOT).astype(BF16)
    spread = jnp.where(iota((groups, rows), 1) // BLOCK == iota((groups, rows), 0), 1.0, 0.0).astype(BF16)
    keys = dot(key, spread)
    coarse = factor.astype(BF16)
    fine = (factor - coarse.astype(F32)).astype(BF16)
    coarse, fine = dot(coarse, spread), dot(fine, spread)
    place = iota((tokens, rows), 1)
    on_time = keys == (place % BLOCK).astype(F32)
    late = keys == (BLOCK + (place % BLOCK) // 4).astype(F32)

    def weighted(mask, rows_back):
        a = jnp.where(mask, coarse, 0.0).astype(BF16)
        b = jnp.where(mask, fine, 0.0).astype(BF16)
        return dot(a, rows_back) + dot(b, rows_back)

    for first, target in ((0, moe_ref), (width + part, sum_ref)):
        target[...] = weighted(on_time, back_ref[:, first : first + width])
        tail = back_ref[:, first + width : first + width + part]
        for k in range(4):
            target[:, k * part : (k + 1) * part] += weighted(late & (place % 4 == k), tail)
    stream = stream_ref[...]
    mixed_ref[...] = (stream + moe_ref[...]).astype(BF16)
    scale_back = lax.rsqrt(jnp.mean(stream * stream, -1, keepdims=True) + 1e-06)
    gain_grad = gain_ref[...] * sum_ref[...]
    inner = jnp.mean(stream * gain_grad, -1, keepdims=True)
    grad_ref[...] = cot_ref[...].astype(F32) + scale_back * gain_grad - stream * (scale_back**3 * inner)


def on_device(
    queries,
    key_rows,
    values,
    residual,
    seg_lengths,
    seg_parent,
    ln_gain,
    w_gate,
    w_up,
    w_down,
    expert_ids,
    gate_weights,
    cotangent,
):
    groups = lax.axis_size("exp")
    members = lax.axis_size("ctx")
    tokens, width = residual.shape[1], residual.shape[2]
    kv_width = key_rows.shape[2] + values.shape[2]
    hidden = w_gate.shape[2]
    slab = members * tokens
    rows = groups * BLOCK
    packed = width + width // 4
    shape = jax.ShapeDtypeStruct
    me = lax.axis_index("ctx").astype(jnp.int32).reshape(1)
    ids_t = expert_ids[0].T
    gain = ln_gain.reshape(1, width)

    kv, w_own = call(pack_body, (shape((tokens, kv_width), BF16), shape((tokens, 3 * hidden), BF16)))(
        key_rows[0], values[0], w_gate[0], w_up[0], w_down[0]
    )

    def send(rows_out, target):
        return lax.ppermute(rows_out, "ctx", [(i, target(i)) for i in range(members)])

    def along_x(i, step):
        return (i // 4 + step) % 4 * 4 + i % 4

    pair = send(kv, lambda i: i ^ 2)
    both = jnp.concatenate([kv, pair], 0)
    near, far, last = (send(both, functools.partial(along_x, step=step)) for step in (1, 2, 3))
    mine = jnp.concatenate([both, near, far, last], 0)
    other_core = send(mine, lambda i: i ^ 1)

    weights = lax.all_gather(w_own, "ctx", axis=0, tiled=True)

    in_smem = pl.BlockSpec(memory_space=pltpu.SMEM)
    in_vmem = pl.BlockSpec(memory_space=pltpu.VMEM)
    bias, send_grad = pl.pallas_call(
        functools.partial(prepare_body, groups),
        out_shape=(shape((tokens, slab), F32), shape((rows, packed), BF16)),
        in_specs=[in_smem] + [in_vmem] * 5,
        out_specs=(in_vmem, in_vmem),
        compiler_params=pltpu.CompilerParams(vmem_limit_bytes=48 << 20),
    )(me, cotangent[0], ids_t, seg_lengths, seg_lengths.reshape(-1, 1), seg_parent.reshape(-1, 1))

    def exchange(sent):
        return lax.all_to_all(
            sent.reshape(groups, BLOCK, sent.shape[1]), "exp", split_axis=0, concat_axis=0, tiled=True
        ).reshape(sent.shape)

    arrived_grad = exchange(send_grad)
    stream, send_input = call(
        functools.partial(attend_body, groups),
        (shape((tokens, width), F32), shape((rows, packed), BF16)),
        [pltpu.VMEM((slab, kv_width), BF16)],
        flops=4 * tokens * slab * width,
        moved=8 << 20,
    )(queries[0], kv, pair, near, far, last, other_core, bias, residual[0], gain, ids_t)
    arrived_in = exchange(send_input)
    returned = call(
        expert_body,
        shape((rows, 2 * packed), BF16),
        [pltpu.VMEM((groups * CAP, width), BF16)] * 2,
        flops=12 * groups * CAP * width * hidden,
        moved=10 << 20,
    )(arrived_in, arrived_grad, weights)
    back = exchange(returned)
    mixed_out, stream_grad = call(
        functools.partial(combine_body, groups),
        (shape((tokens, width), BF16), shape((tokens, width), F32)),
        [pltpu.VMEM((tokens, width), F32)] * 2,
    )(back, stream, cotangent[0], gain, expert_ids[0], gate_weights[0])
    return (mixed_out[None], stream_grad[None])


def solution(mesh):
    placed = (
        P("exp", "ctx", None),
        P("exp", "ctx", None),
        P("exp", "ctx", None),
        P("exp", "ctx", None),
        P("exp", None),
        P("exp", None),
        P(),
        P("exp", "ctx", None),
        P("exp", "ctx", None),
        P("exp", None, "ctx"),
        P("exp", "ctx", None),
        P("exp", "ctx", None),
        P("exp", "ctx", None),
    )
    return jax.shard_map(
        on_device,
        mesh=mesh,
        in_specs=placed,
        out_specs=(P("exp", "ctx", None), P("exp", "ctx", None)),
        check_vma=False,
    )
```

```python
import functools
import math

import jax
import jax.numpy as jnp
from jax import lax
from jax.experimental import pallas as pl
from jax.experimental.pallas import tpu as pltpu
from jax.sharding import PartitionSpec as P

HEAD_DIM = 128
TOPK = 8
CAP = 10
BLOCK = 8
NO_SLOT = 512.0
TOGETHER = 4
ROOMY = 28 << 20
ALONE = 60 << 20
HIDDEN = -1e30
F32 = jnp.float32
BF16 = jnp.bfloat16
NT = (((1,), (1,)), ((), ()))


def iota(shape, dim):
    return lax.broadcasted_iota(jnp.int32, shape, dim)


def dot(a, b):
    return jnp.dot(a, b, preferred_element_type=F32)


def dot_nt(a, b):
    return lax.dot_general(a, b, NT, preferred_element_type=F32)


def call(body, outs, scratch=(), in_specs=None, out_specs=None, flops=0, moved=0, vmem=ALONE):
    specs = {} if in_specs is None else {"in_specs": in_specs, "out_specs": out_specs}
    return pl.pallas_call(
        body,
        out_shape=outs,
        **specs,
        scratch_shapes=list(scratch),
        compiler_params=pltpu.CompilerParams(vmem_limit_bytes=vmem),
        cost_estimate=pl.CostEstimate(flops=flops, bytes_accessed=moved, transcendentals=0),
    )


def slot_keys(ids_t, groups):
    tokens = ids_t.shape[1]
    group = iota((groups, tokens), 0)
    named = jnp.zeros((groups, tokens), F32)
    for route in range(ids_t.shape[0]):
        named = named + jnp.where(ids_t[route : route + 1, :] == group, 1.0, 0.0)
    before = (iota((tokens, tokens), 0) < iota((tokens, tokens), 1)).astype(F32)
    rank = dot(named.astype(BF16), before.astype(BF16))
    key = jnp.where(named > 0.5, rank, NO_SLOT).astype(BF16)
    rows = groups * BLOCK
    spread = (iota((rows, groups), 0) // BLOCK == iota((rows, groups), 1)).astype(F32)
    return dot(spread.astype(BF16), key)


def dispatch(rows, keys, out_ref):
    place = iota(keys.shape, 0)
    width = rows.shape[1]
    part = width // 4
    pick = jnp.where(keys == (place % BLOCK).astype(F32), 1.0, 0.0).astype(BF16)
    out_ref[:, :width] = dot(pick, rows).astype(BF16)
    late = keys == (BLOCK + (place % BLOCK) // 4).astype(F32)
    tail = jnp.zeros((keys.shape[0], part), F32)
    for k in range(4):
        pick = jnp.where(late & (place % 4 == k), 1.0, 0.0).astype(BF16)
        tail = tail + dot(pick, rows[:, k * part : (k + 1) * part])
    out_ref[:, width:] = tail.astype(BF16)


def copy_all(copies):
    for one in copies:
        one.start()
    for one in copies:
        one.wait()


def pack_kv_body(key_hbm, value_hbm, kv_hbm, kv_ref, sems):
    half = key_hbm.shape[1]
    copy_all(
        [
            pltpu.make_async_copy(key_hbm, kv_ref.at[:, pl.ds(0, half)], sems.at[0]),
            pltpu.make_async_copy(value_hbm, kv_ref.at[:, pl.ds(half, half)], sems.at[1]),
        ]
    )
    copy_all([pltpu.make_async_copy(kv_ref, kv_hbm, sems.at[2])])


def pack_w_body(gate_hbm, up_hbm, down_hbm, w_hbm, down_ref, w_ref, sems):
    hidden = gate_hbm.shape[1]
    copies = [
        pltpu.make_async_copy(down_hbm, down_ref, sems.at[0]),
        pltpu.make_async_copy(gate_hbm, w_ref.at[:, pl.ds(0, hidden)], sems.at[1]),
        pltpu.make_async_copy(up_hbm, w_ref.at[:, pl.ds(hidden, hidden)], sems.at[2]),
    ]
    copy_all(copies)
    w_ref[:, 2 * hidden :] = down_ref[...].T
    copy_all([pltpu.make_async_copy(w_ref, w_hbm, sems.at[3])])


def place_of(me, n):
    x, y, core = me // 4, (me // 2) % 2, me % 2
    return (x + 4 - n % 8 // 2) % 4 * 4 + (y + n) % 2 * 2 + (core + n // 8) % 2


def stack_body(count, *refs):
    out_ref, sems = refs[-2:]
    first, copies = 0, []
    for n, piece in enumerate(refs[:count]):
        copies.append(pltpu.make_async_copy(piece, out_ref.at[pl.ds(first, piece.shape[0])], sems.at[n]))
        first += piece.shape[0]
    copy_all(copies)


def tie_body(array_ref, after_ref, out_ref):
    del array_ref, after_ref, out_ref


def scatter_body(groups, rows_hbm, ids_hbm, send_hbm, rows_ref, ids_ref, send_ref, sems):
    get_ids = pltpu.make_async_copy(ids_hbm, ids_ref, sems.at[0])
    get_rows = pltpu.make_async_copy(rows_hbm, rows_ref, sems.at[1])
    get_ids.start()
    get_rows.start()
    get_ids.wait()
    keys = slot_keys(ids_ref[...], groups)
    get_rows.wait()
    dispatch(rows_ref[...], keys, send_ref)
    copy_all([pltpu.make_async_copy(send_ref, send_hbm, sems.at[2])])


def bias_body(me_ref, len_hbm, parent_hbm, bias_hbm, len_ref, parent_ref, bias_ref, sems):
    copy_all(
        [
            pltpu.make_async_copy(len_hbm, len_ref, sems.at[0]),
            pltpu.make_async_copy(parent_hbm, parent_ref, sems.at[1]),
        ]
    )
    segs = len_ref.shape[1]
    rows = bias_ref.shape[0]
    low, high = iota((segs, segs), 0), iota((segs, segs), 1)
    len_row = len_ref[...].astype(F32)
    len_col = jnp.sum(jnp.where(low == high, len_row, 0.0), 1, keepdims=True)
    parent_col = jnp.sum(jnp.where(low == high, parent_ref[...].astype(F32), 0.0), 1, keepdims=True)
    start_col = jnp.sum(jnp.where(high < low, len_row, 0.0), 1, keepdims=True)
    start_row = jnp.sum(jnp.where(low < high, len_col, 0.0), 0, keepdims=True)
    finish_col = start_col + len_col
    finish_row = start_row + len_row
    reached = jnp.where((parent_col == high.astype(F32)) | (low == high), 1.0, 0.0)
    for sweep in range(max(1, (segs - 1).bit_length())):
        low_bits = reached.astype(BF16)
        reached = jnp.minimum(dot(low_bits, low_bits), 1.0)
    me = me_ref[0]
    query_pos = (me * rows + iota((rows, 1), 0)).astype(F32)
    member = jnp.where((query_pos >= start_row) & (query_pos < finish_row), 1.0, 0.0)
    query_reach = dot(member.astype(BF16), reached.astype(BF16)).astype(BF16)
    for n in range(bias_ref.shape[1] // rows):
        key_pos = (place_of(me, n) * rows + iota((1, rows), 1)).astype(F32)
        holds = jnp.where((key_pos >= start_col) & (key_pos < finish_col), 1.0, 0.0)
        linked = dot(query_reach, holds.astype(BF16))
        visible = (linked > 0.5) & (key_pos <= query_pos)
        bias_ref[:, n * rows : (n + 1) * rows] = jnp.where(visible, 0.0, HIDDEN)
    copy_all([pltpu.make_async_copy(bias_ref, bias_hbm, sems.at[2])])


def attend_body(
    groups,
    q_hbm,
    mine_hbm,
    core_hbm,
    residual_hbm,
    bias_hbm,
    gain_hbm,
    ids_hbm,
    stream_hbm,
    send_hbm,
    q_ref,
    kv_ref,
    residual_ref,
    bias_ref,
    gain_ref,
    ids_ref,
    stream_ref,
    send_ref,
    sems,
):
    pieces, first, fetch = (mine_hbm, core_hbm), 0, []
    for n, piece in enumerate(pieces):
        fetch.append(pltpu.make_async_copy(piece, kv_ref.at[pl.ds(first, piece.shape[0])], sems.at[n]))
        first += piece.shape[0]
    fetch += [
        pltpu.make_async_copy(q_hbm, q_ref, sems.at[2]),
        pltpu.make_async_copy(bias_hbm, bias_ref, sems.at[3]),
        pltpu.make_async_copy(residual_hbm, residual_ref, sems.at[6]),
        pltpu.make_async_copy(gain_hbm, gain_ref, sems.at[7]),
        pltpu.make_async_copy(ids_hbm, ids_ref, sems.at[8]),
    ]
    for one in fetch:
        one.start()
    for one in fetch[:4]:
        one.wait()
    kv_heads = kv_ref.shape[1] // (2 * HEAD_DIM)
    per_kv = q_ref.shape[1] // HEAD_DIM // kv_heads
    factor = HEAD_DIM**-0.5 * math.log2(math.e)
    for g in range(kv_heads):
        keys = kv_ref[:, g * HEAD_DIM : (g + 1) * HEAD_DIM]
        vals = kv_ref[:, (kv_heads + g) * HEAD_DIM : (kv_heads + g + 1) * HEAD_DIM]

        def heads(i, carry):
            at = [pl.multiple_of((g * per_kv + i * TOGETHER + j) * HEAD_DIM, HEAD_DIM) for j in range(TOGETHER)]
            scores = [dot_nt(q_ref[:, pl.ds(a, HEAD_DIM)], keys) + bias_ref[...] for a in at]
            for a, score in zip(at, scores):
                top = jnp.max(score, -1, keepdims=True)
                probs = jnp.exp2((score - top) * factor)
                denom = jnp.sum(probs, -1, keepdims=True)
                attended = (dot(probs.astype(BF16), vals) / denom).astype(BF16)
                stream_ref[:, pl.ds(a, HEAD_DIM)] = attended.astype(F32)
            return carry

        lax.fori_loop(0, per_kv // TOGETHER, heads, 0)
    for one in fetch[4:]:
        one.wait()
    stream = residual_ref[...].astype(F32) + stream_ref[...]
    stream_ref[...] = stream
    keep = pltpu.make_async_copy(stream_ref, stream_hbm, sems.at[4])
    keep.start()
    scale_back = lax.rsqrt(jnp.mean(stream * stream, -1, keepdims=True) + 1e-06)
    normed = (stream * scale_back * gain_ref[...]).astype(BF16)
    dispatch(normed, slot_keys(ids_ref[...], groups), send_ref)
    out = pltpu.make_async_copy(send_ref, send_hbm, sems.at[5])
    out.start()
    keep.wait()
    out.wait()


def expert_body(me_ref, rows_hbm, grads_hbm, *refs):
    out_hbm, x_ref, x_tail, g_ref, g_tail, w_ref, out_ref, sems, w_sems, out_sems = refs[-10:]
    width = w_ref.shape[0]
    hidden = w_ref.shape[1] // 3
    main = rows_hbm.shape[0]
    part = width // 4
    tails = main // 4
    blocks = w_sems.shape[1]
    tall = width // blocks
    pieces = [(piece, row) for piece in refs[:-10] for row in range(0, piece.shape[0], tall)]

    def fetch_rows(source, whole, tail, first):
        return [
            pltpu.make_async_copy(source.at[:, pl.ds(0, width)], whole.at[pl.ds(0, main)], sems.at[first]),
            pltpu.make_async_copy(source.at[:, pl.ds(width, part)], tail, sems.at[first + 1]),
        ]

    def fetch_weights(group, first, wide):
        copies = []
        for n in range(blocks):
            piece, row = pieces[n]
            source = piece.at[pl.ds(row, tall), pl.ds(first, wide)]
            rows = pl.ds(pl.multiple_of(place_of(me_ref[0], n) * tall, tall), tall)
            copies.append(pltpu.make_async_copy(source, w_ref.at[rows, pl.ds(first, wide)], w_sems.at[group, n]))
        return copies

    get_rows = fetch_rows(rows_hbm, x_ref, x_tail, 0)
    get_grads = fetch_rows(grads_hbm, g_ref, g_tail, 2)
    get_in = fetch_weights(0, 0, 2 * hidden)
    get_out = fetch_weights(1, 2 * hidden, hidden)
    for one in get_rows + get_in + get_out + get_grads:
        one.start()

    def unpack(tail, target):
        at = iota((tails, main), 1) - 4 * iota((tails, main), 0)
        for k in range(4):
            pick = jnp.where(at == k, 1.0, 0.0).astype(BF16)
            target[main:, k * part : (k + 1) * part] = dot(pick, tail[...]).astype(BF16)

    def pack(rows, index):
        first = index * (width + part)
        out_ref[:, first : first + width] = rows[:main, :]
        at = iota((main, tails), 0) - 4 * iota((main, tails), 1)
        tail = jnp.zeros((main, part), F32)
        for k in range(4):
            pick = jnp.where(at == k, 1.0, 0.0).astype(BF16)
            tail = tail + dot(pick, rows[main:, k * part : (k + 1) * part])
        out_ref[:, first + width : first + width + part] = tail.astype(BF16)
        columns = pl.ds(first, width + part)
        copy = pltpu.make_async_copy(out_ref.at[:, columns], out_hbm.at[:, columns], out_sems.at[index])
        copy.start()
        return copy

    for one in get_rows:
        one.wait()
    unpack(x_tail, x_ref)
    for one in get_in:
        one.wait()
    both = dot(x_ref[...], w_ref[:, : 2 * hidden])
    gate, up = both[:, :hidden], both[:, hidden:]
    sig = jax.nn.sigmoid(gate)
    silu = gate * sig
    activated = (silu * up).astype(BF16)
    for one in get_out:
        one.wait()
    put_out = pack(dot_nt(activated, w_ref[:, 2 * hidden :]).astype(BF16), 0)
    for one in get_grads:
        one.wait()
    unpack(g_tail, g_ref)
    back = dot(g_ref[...], w_ref[:, 2 * hidden :])
    d_gate = (back * up * sig * (1.0 + gate * (1.0 - sig))).astype(BF16)
    d_up = (back * silu).astype(BF16)
    grad = dot_nt(d_gate, w_ref[:, :hidden]) + dot_nt(d_up, w_ref[:, hidden : 2 * hidden])
    put_grad = pack(grad.astype(BF16), 1)
    put_out.wait()
    put_grad.wait()


def factor_body(groups, ids_hbm, weight_hbm, factor_hbm, ids_ref, weight_ref, factor_ref, sems):
    fetch = [
        pltpu.make_async_copy(ids_hbm, ids_ref, sems.at[0]),
        pltpu.make_async_copy(weight_hbm, weight_ref, sems.at[1]),
    ]
    copy_all(fetch)
    tokens = ids_ref.shape[1]
    rows = groups * BLOCK
    group = iota((groups, tokens), 0)
    factor = jnp.zeros((groups, tokens), F32)
    for route in range(ids_ref.shape[0]):
        here = ids_ref[route : route + 1, :] == group
        factor = factor + jnp.where(here, weight_ref[route : route + 1, :], 0.0)
    spread = jnp.where(iota((rows, groups), 0) // BLOCK == iota((rows, groups), 1), 1.0, 0.0).astype(BF16)
    coarse = factor.astype(BF16)
    fine = (factor - coarse.astype(F32)).astype(BF16)
    keys = slot_keys(ids_ref[...], groups).T
    coarse, fine = dot(spread, coarse).T, dot(spread, fine).T
    place = iota((tokens, rows), 1)
    late = keys == (BLOCK + (place % BLOCK) // 4).astype(F32)
    masks = [keys == (place % BLOCK).astype(F32)] + [late & (place % 4 == k) for k in range(4)]
    for n, mask in enumerate(masks):
        factor_ref[:, 2 * n * rows : (2 * n + 1) * rows] = jnp.where(mask, coarse, 0.0).astype(BF16)
        factor_ref[:, (2 * n + 1) * rows : (2 * n + 2) * rows] = jnp.where(mask, fine, 0.0).astype(BF16)
    copy_all([pltpu.make_async_copy(factor_ref, factor_hbm, sems.at[2])])


def combine_body(
    back_hbm, stream_hbm, cot_hbm, gain_hbm, factor_hbm, mixed_hbm, grad_hbm,
    back_ref, stream_ref, cot_ref, gain_ref, factor_ref, mixed_ref, moe_ref, sum_ref, sems, in_sems,
):
    packed = back_hbm.shape[1] // 2
    halves = [
        pltpu.make_async_copy(
            back_hbm.at[:, pl.ds(i * packed, packed)], back_ref.at[:, pl.ds(i * packed, packed)], sems.at[i]
        )
        for i in range(2)
    ]
    others = [
        pltpu.make_async_copy(source, target, in_sems.at[n])
        for n, (source, target) in enumerate(
            ((factor_hbm, factor_ref), (stream_hbm, stream_ref), (cot_hbm, cot_ref), (gain_hbm, gain_ref))
        )
    ]
    for one in others[:1] + halves[:1] + others[1:] + halves[1:]:
        one.start()
    width = stream_hbm.shape[1]
    part = width // 4
    rows = back_hbm.shape[0]
    others[0].wait()

    def weighted(n, rows_back):
        a = factor_ref[:, 2 * n * rows : (2 * n + 1) * rows]
        b = factor_ref[:, (2 * n + 1) * rows : (2 * n + 2) * rows]
        return dot(a, rows_back) + dot(b, rows_back)

    def gather(index, target):
        halves[index].wait()
        first = index * packed
        target[...] = weighted(0, back_ref[:, first : first + width])
        tail = back_ref[:, first + width : first + packed]
        for k in range(4):
            target[:, k * part : (k + 1) * part] += weighted(1 + k, tail)

    gather(0, moe_ref)
    for one in others[1:]:
        one.wait()
    stream = stream_ref[...]
    mixed_ref[...] = (stream + moe_ref[...]).astype(BF16)
    put_mixed = pltpu.make_async_copy(mixed_ref, mixed_hbm, sems.at[4])
    put_mixed.start()
    gather(1, sum_ref)
    scale_back = lax.rsqrt(jnp.mean(stream * stream, -1, keepdims=True) + 1e-06)
    gain_grad = gain_ref[...] * sum_ref[...]
    inner = jnp.mean(stream * gain_grad, -1, keepdims=True)
    moe_ref[...] = cot_ref[...].astype(F32) + scale_back * gain_grad - stream * (scale_back**3 * inner)
    put_grad = pltpu.make_async_copy(moe_ref, grad_hbm, sems.at[5])
    put_grad.start()
    put_mixed.wait()
    put_grad.wait()


def on_device(
    queries,
    key_rows,
    values,
    residual,
    seg_lengths,
    seg_parent,
    ln_gain,
    w_gate,
    w_up,
    w_down,
    expert_ids,
    gate_weights,
    cotangent,
):
    groups = lax.axis_size("exp")
    members = lax.axis_size("ctx")
    tokens, width = residual.shape[1], residual.shape[2]
    kv_width = key_rows.shape[2] + values.shape[2]
    hidden = w_gate.shape[2]
    slab = members * tokens
    rows = groups * BLOCK
    packed = width + width // 4
    shape = jax.ShapeDtypeStruct
    me = lax.axis_index("ctx").astype(jnp.int32).reshape(1)
    ids_t = expert_ids[0].T
    gain = ln_gain.reshape(1, width)

    in_smem = pl.BlockSpec(memory_space=pltpu.SMEM)
    anywhere = pl.BlockSpec(memory_space=pl.ANY)
    in_hbm = pl.BlockSpec(memory_space=pltpu.HBM)
    copy_sem = pltpu.SemaphoreType.DMA

    def tie(array, after):
        return pl.pallas_call(
            tie_body,
            out_shape=shape(array.shape, array.dtype),
            in_specs=[anywhere] * 2,
            out_specs=anywhere,
            input_output_aliases={0: 0},
        )(array, after)

    kv = call(
        pack_kv_body,
        shape((tokens, kv_width), BF16),
        [pltpu.VMEM((tokens, kv_width), BF16), copy_sem((3,))],
        [in_hbm] * 2,
        in_hbm,
    )(key_rows[0], values[0])
    w_own = call(
        pack_w_body,
        shape((tokens, 3 * hidden), BF16),
        [pltpu.VMEM(w_down.shape[1:], BF16), pltpu.VMEM((tokens, 3 * hidden), BF16), copy_sem((4,))],
        [in_hbm] * 3,
        in_hbm,
        moved=1 << 20,
    )(w_gate[0], w_up[0], w_down[0])

    def send(rows_out, target):
        return lax.ppermute(rows_out, "ctx", [(i, target(i)) for i in range(members)])

    def along_x(i, step):
        return (i // 4 + step) % 4 * 4 + i % 4

    def cross(rows_out):
        return send(rows_out, lambda i: i ^ 1)

    def stack(pieces, after=()):
        height = sum(piece.shape[0] for piece in pieces)
        return call(
            functools.partial(stack_body, len(pieces)),
            shape((height, pieces[0].shape[1]), BF16),
            [copy_sem((len(pieces),))],
            [in_hbm] * len(pieces) + [anywhere] * len(after),
            in_hbm,
            moved=2 * height * pieces[0].shape[1],
            vmem=ROOMY,
        )(*pieces, *after)

    factors = call(
        functools.partial(factor_body, groups),
        shape((tokens, 10 * rows), BF16),
        [
            pltpu.VMEM(ids_t.shape, jnp.int32),
            pltpu.VMEM(ids_t.shape, F32),
            pltpu.VMEM((tokens, 10 * rows), BF16),
            copy_sem((3,)),
        ],
        [in_hbm] * 2,
        in_hbm,
        moved=1 << 20,
    )(ids_t, gate_weights[0].T)
    bias = call(
        bias_body,
        shape((tokens, slab), F32),
        [
            pltpu.VMEM(seg_lengths.shape, jnp.int32),
            pltpu.VMEM(seg_parent.shape, jnp.int32),
            pltpu.VMEM((tokens, slab), F32),
            copy_sem((3,)),
        ],
        [in_smem] + [in_hbm] * 2,
        in_hbm,
        moved=1 << 20,
    )(me, seg_lengths, seg_parent)
    send_grad = call(
        functools.partial(scatter_body, groups),
        shape((rows, packed), BF16),
        [
            pltpu.VMEM((tokens, width), BF16),
            pltpu.VMEM(ids_t.shape, jnp.int32),
            pltpu.VMEM((rows, packed), BF16),
            copy_sem((3,)),
        ],
        [in_hbm] * 2,
        in_hbm,
        flops=2 * rows * tokens * width,
        moved=2 << 20,
    )(cotangent[0], ids_t)

    w_pair = send(w_own, lambda i: i ^ 2)
    kv_both = stack([kv, send(kv, lambda i: i ^ 2)])
    kv_near, kv_far, kv_last = (send(kv_both, functools.partial(along_x, step=step)) for step in (1, 2, 3))
    kv_mine = stack([kv_both, kv_near, kv_far, kv_last], [w_own, factors, bias])
    kv_core = cross(kv_mine)

    def exchange(sent):
        return lax.all_to_all(
            sent.reshape(groups, BLOCK, sent.shape[1]), "exp", split_axis=0, concat_axis=0, tiled=True
        ).reshape(sent.shape)

    arrived_grad = exchange(send_grad)
    stream, send_input = call(
        functools.partial(attend_body, groups),
        (shape((tokens, width), F32), shape((rows, packed), BF16)),
        [
            pltpu.VMEM((tokens, width), BF16),
            pltpu.VMEM((slab, kv_width), BF16),
            pltpu.VMEM((tokens, width), BF16),
            pltpu.VMEM((tokens, slab), F32),
            pltpu.VMEM((1, width), F32),
            pltpu.VMEM(ids_t.shape, jnp.int32),
            pltpu.VMEM((tokens, width), F32),
            pltpu.VMEM((rows, packed), BF16),
            copy_sem((9,)),
        ],
        [in_hbm] * 7,
        (in_hbm, in_hbm),
        flops=24 * tokens * slab * width,
        moved=8 << 20,
    )(queries[0], kv_mine, kv_core, residual[0], bias, gain, ids_t)
    send_input = tie(send_input, w_pair)
    arrived_in = exchange(send_input)
    w_both = stack([w_own, w_pair], [send_input])
    w_near = send(w_both, functools.partial(along_x, step=1))
    w_last = send(w_both, functools.partial(along_x, step=3))
    w_far_own = send(w_near[:tokens], functools.partial(along_x, step=1))
    w_far_pair = send(w_last[tokens:], functools.partial(along_x, step=3))
    w_pieces = [w_both, w_near, w_far_own, w_far_pair, w_last]
    w_pieces = w_pieces + [cross(piece) for piece in w_pieces]
    returned = call(
        expert_body,
        shape((rows, 2 * packed), BF16),
        [
            pltpu.VMEM((groups * CAP, width), BF16),
            pltpu.VMEM((rows, packed - width), BF16),
            pltpu.VMEM((groups * CAP, width), BF16),
            pltpu.VMEM((rows, packed - width), BF16),
            pltpu.VMEM((width, 3 * hidden), BF16),
            pltpu.VMEM((rows, 2 * packed), BF16),
            copy_sem((4,)),
            copy_sem((2, members)),
            copy_sem((2,)),
        ],
        [in_smem] + [in_hbm] * (2 + len(w_pieces)),
        in_hbm,
        flops=12 * groups * CAP * width * hidden,
        moved=10 << 20,
    )(me, arrived_in, arrived_grad, *w_pieces)
    back = exchange(returned)
    mixed_out, stream_grad = call(
        combine_body,
        (shape((tokens, width), BF16), shape((tokens, width), F32)),
        [
            pltpu.VMEM((rows, 2 * packed), BF16),
            pltpu.VMEM((tokens, width), F32),
            pltpu.VMEM((tokens, width), BF16),
            pltpu.VMEM((1, width), F32),
            pltpu.VMEM((tokens, 10 * rows), BF16),
            pltpu.VMEM((tokens, width), BF16),
            pltpu.VMEM((tokens, width), F32),
            pltpu.VMEM((tokens, width), F32),
            copy_sem((6,)),
            copy_sem((4,)),
        ],
        [in_hbm] * 5,
        (in_hbm, in_hbm),
    )(back, stream, cotangent[0], gain, factors)
    return (mixed_out[None], stream_grad[None])


def solution(mesh):
    placed = (
        P("exp", "ctx", None),
        P("exp", "ctx", None),
        P("exp", "ctx", None),
        P("exp", "ctx", None),
        P("exp", None),
        P("exp", None),
        P(),
        P("exp", "ctx", None),
        P("exp", "ctx", None),
        P("exp", None, "ctx"),
        P("exp", "ctx", None),
        P("exp", "ctx", None),
        P("exp", "ctx", None),
    )
    return jax.shard_map(
        on_device,
        mesh=mesh,
        in_specs=placed,
        out_specs=(P("exp", "ctx", None), P("exp", "ctx", None)),
        check_vma=False,
    )
```

```python
import functools
import math

import jax
import jax.numpy as jnp
from jax import lax
from jax.experimental import pallas as pl
from jax.experimental.pallas import tpu as pltpu
from jax.sharding import PartitionSpec as P

HEAD_DIM = 128
TOPK = 8
CAP = 10
BLOCK = 8
NO_SLOT = 512.0
TOGETHER = 8
ROOMY = 28 << 20
ALONE = 60 << 20
HIDDEN = -1e30
F32 = jnp.float32
BF16 = jnp.bfloat16
NT = (((1,), (1,)), ((), ()))


def iota(shape, dim):
    return lax.broadcasted_iota(jnp.int32, shape, dim)


def dot(a, b):
    return jnp.dot(a, b, preferred_element_type=F32)


def dot_nt(a, b):
    return lax.dot_general(a, b, NT, preferred_element_type=F32)


def call(body, outs, scratch=(), in_specs=None, out_specs=None, flops=0, moved=0, vmem=ALONE):
    specs = {} if in_specs is None else {"in_specs": in_specs, "out_specs": out_specs}
    return pl.pallas_call(
        body,
        out_shape=outs,
        **specs,
        scratch_shapes=list(scratch),
        compiler_params=pltpu.CompilerParams(vmem_limit_bytes=vmem),
        cost_estimate=pl.CostEstimate(flops=flops, bytes_accessed=moved, transcendentals=0),
    )


def slot_keys(ids_t, groups):
    tokens = ids_t.shape[1]
    group = iota((groups, tokens), 0)
    named = jnp.zeros((groups, tokens), F32)
    for route in range(ids_t.shape[0]):
        named = named + jnp.where(ids_t[route : route + 1, :] == group, 1.0, 0.0)
    before = (iota((tokens, tokens), 0) < iota((tokens, tokens), 1)).astype(F32)
    rank = dot(named.astype(BF16), before.astype(BF16))
    key = jnp.where(named > 0.5, rank, NO_SLOT).astype(BF16)
    rows = groups * BLOCK
    spread = (iota((rows, groups), 0) // BLOCK == iota((rows, groups), 1)).astype(F32)
    return dot(spread.astype(BF16), key)


def dispatch(rows, keys, out_ref):
    place = iota(keys.shape, 0)
    width = rows.shape[1]
    part = width // 4
    pick = jnp.where(keys == (place % BLOCK).astype(F32), 1.0, 0.0).astype(BF16)
    out_ref[:, :width] = dot(pick, rows).astype(BF16)
    late = keys == (BLOCK + (place % BLOCK) // 4).astype(F32)
    tail = jnp.zeros((keys.shape[0], part), F32)
    for k in range(4):
        pick = jnp.where(late & (place % 4 == k), 1.0, 0.0).astype(BF16)
        tail = tail + dot(pick, rows[:, k * part : (k + 1) * part])
    out_ref[:, width:] = tail.astype(BF16)


def copy_all(copies):
    for one in copies:
        one.start()
    for one in copies:
        one.wait()


def pack_kv_body(key_hbm, value_hbm, kv_hbm, kv_ref, sems):
    half = key_hbm.shape[1]
    copy_all(
        [
            pltpu.make_async_copy(key_hbm, kv_ref.at[:, pl.ds(0, half)], sems.at[0]),
            pltpu.make_async_copy(value_hbm, kv_ref.at[:, pl.ds(half, half)], sems.at[1]),
        ]
    )
    copy_all([pltpu.make_async_copy(kv_ref, kv_hbm, sems.at[2])])


def pack_w_body(gate_hbm, up_hbm, down_hbm, w_hbm, down_ref, w_ref, sems):
    hidden = gate_hbm.shape[1]
    copies = [
        pltpu.make_async_copy(down_hbm, down_ref, sems.at[0]),
        pltpu.make_async_copy(gate_hbm, w_ref.at[:, pl.ds(0, hidden)], sems.at[1]),
        pltpu.make_async_copy(up_hbm, w_ref.at[:, pl.ds(hidden, hidden)], sems.at[2]),
    ]
    copy_all(copies)
    w_ref[:, 2 * hidden :] = down_ref[...].T
    copy_all([pltpu.make_async_copy(w_ref, w_hbm, sems.at[3])])


def place_of(me, n):
    x, y, core = me // 4, (me // 2) % 2, me % 2
    return (x + 4 - n % 8 // 2) % 4 * 4 + (y + n) % 2 * 2 + (core + n // 8) % 2


def stack_body(count, *refs):
    out_ref, sems = refs[-2:]
    first, copies = 0, []
    for n, piece in enumerate(refs[:count]):
        copies.append(pltpu.make_async_copy(piece, out_ref.at[pl.ds(first, piece.shape[0])], sems.at[n]))
        first += piece.shape[0]
    copy_all(copies)


def scatter_body(groups, rows_hbm, ids_hbm, send_hbm, rows_ref, ids_ref, send_ref, sems):
    get_ids = pltpu.make_async_copy(ids_hbm, ids_ref, sems.at[0])
    get_rows = pltpu.make_async_copy(rows_hbm, rows_ref, sems.at[1])
    get_ids.start()
    get_rows.start()
    get_ids.wait()
    keys = slot_keys(ids_ref[...], groups)
    get_rows.wait()
    dispatch(rows_ref[...], keys, send_ref)
    copy_all([pltpu.make_async_copy(send_ref, send_hbm, sems.at[2])])


def bias_body(me_ref, len_hbm, parent_hbm, bias_hbm, len_ref, parent_ref, bias_ref, sems, put_sem):
    copy_all(
        [
            pltpu.make_async_copy(len_hbm, len_ref, sems.at[0]),
            pltpu.make_async_copy(parent_hbm, parent_ref, sems.at[1]),
        ]
    )
    segs = len_ref.shape[1]
    rows = bias_ref.shape[0]
    low, high = iota((segs, segs), 0), iota((segs, segs), 1)
    len_row = len_ref[...].astype(F32)
    len_col = jnp.sum(jnp.where(low == high, len_row, 0.0), 1, keepdims=True)
    parent_col = jnp.sum(jnp.where(low == high, parent_ref[...].astype(F32), 0.0), 1, keepdims=True)
    start_col = jnp.sum(jnp.where(high < low, len_row, 0.0), 1, keepdims=True)
    start_row = jnp.sum(jnp.where(low < high, len_col, 0.0), 0, keepdims=True)
    finish_col = start_col + len_col
    finish_row = start_row + len_row
    reached = jnp.where((parent_col == high.astype(F32)) | (low == high), 1.0, 0.0)
    for sweep in range(max(1, (segs - 1).bit_length())):
        low_bits = reached.astype(BF16)
        reached = jnp.minimum(dot(low_bits, low_bits), 1.0)
    me = me_ref[0]
    query_pos = (me * rows + iota((rows, 1), 0)).astype(F32)
    member = jnp.where((query_pos >= start_row) & (query_pos < finish_row), 1.0, 0.0)
    query_reach = dot(member.astype(BF16), reached.astype(BF16)).astype(BF16)
    for n in range(bias_ref.shape[1] // rows):
        key_pos = (place_of(me, n) * rows + iota((1, rows), 1)).astype(F32)
        holds = jnp.where((key_pos >= start_col) & (key_pos < finish_col), 1.0, 0.0)
        linked = dot(query_reach, holds.astype(BF16))
        visible = (linked > 0.5) & (key_pos <= query_pos)
        bias_ref[:, n * rows : (n + 1) * rows] = jnp.where(visible, 0.0, HIDDEN)
    put = pltpu.make_async_copy(bias_ref, bias_hbm, put_sem.at[0])
    put.start()
    return put


def attend_body(
    groups,
    q_hbm,
    mine_hbm,
    core_hbm,
    residual_hbm,
    bias_hbm,
    gain_hbm,
    ids_hbm,
    stream_hbm,
    send_hbm,
    q_ref,
    kv_ref,
    residual_ref,
    bias_ref,
    gain_ref,
    ids_ref,
    stream_ref,
    send_ref,
    sems,
):
    pieces, first, fetch = (mine_hbm, core_hbm), 0, []
    for n, piece in enumerate(pieces):
        fetch.append(pltpu.make_async_copy(piece, kv_ref.at[pl.ds(first, piece.shape[0])], sems.at[n]))
        first += piece.shape[0]
    fetch += [
        pltpu.make_async_copy(q_hbm, q_ref, sems.at[2]),
        pltpu.make_async_copy(bias_hbm, bias_ref, sems.at[3]),
        pltpu.make_async_copy(residual_hbm, residual_ref, sems.at[6]),
        pltpu.make_async_copy(gain_hbm, gain_ref, sems.at[7]),
        pltpu.make_async_copy(ids_hbm, ids_ref, sems.at[8]),
    ]
    for one in fetch:
        one.start()
    for one in fetch[:4]:
        one.wait()
    kv_heads = kv_ref.shape[1] // (2 * HEAD_DIM)
    per_kv = q_ref.shape[1] // HEAD_DIM // kv_heads
    factor = HEAD_DIM**-0.5 * math.log2(math.e)
    for g in range(kv_heads):
        keys = kv_ref[:, g * HEAD_DIM : (g + 1) * HEAD_DIM]
        vals = kv_ref[:, (kv_heads + g) * HEAD_DIM : (kv_heads + g + 1) * HEAD_DIM]

        def heads(i, carry):
            at = [pl.multiple_of((g * per_kv + i * TOGETHER + j) * HEAD_DIM, HEAD_DIM) for j in range(TOGETHER)]
            scores = [dot_nt(q_ref[:, pl.ds(a, HEAD_DIM)], keys) + bias_ref[...] for a in at]
            for a, score in zip(at, scores):
                top = jnp.max(score, -1, keepdims=True)
                probs = jnp.exp2((score - top) * factor)
                denom = jnp.sum(probs, -1, keepdims=True)
                attended = (dot(probs.astype(BF16), vals) / denom).astype(BF16)
                stream_ref[:, pl.ds(a, HEAD_DIM)] = attended.astype(F32)
            return carry

        lax.fori_loop(0, per_kv // TOGETHER, heads, 0)
    for one in fetch[4:]:
        one.wait()
    stream = residual_ref[...].astype(F32) + stream_ref[...]
    stream_ref[...] = stream
    keep = pltpu.make_async_copy(stream_ref, stream_hbm, sems.at[4])
    keep.start()
    scale_back = lax.rsqrt(jnp.mean(stream * stream, -1, keepdims=True) + 1e-06)
    normed = (stream * scale_back * gain_ref[...]).astype(BF16)
    dispatch(normed, slot_keys(ids_ref[...], groups), send_ref)
    out = pltpu.make_async_copy(send_ref, send_hbm, sems.at[5])
    out.start()
    keep.wait()
    out.wait()


def expert_body(me_ref, rows_hbm, grads_hbm, *refs):
    out_hbm, x_ref, x_tail, g_ref, g_tail, w_ref, out_ref, sems, w_sems, out_sems = refs[-10:]
    width = w_ref.shape[0]
    hidden = w_ref.shape[1] // 3
    main = rows_hbm.shape[0]
    part = width // 4
    tails = main // 4
    blocks = w_sems.shape[1]
    tall = width // blocks
    pieces = [(piece, row) for piece in refs[:-10] for row in range(0, piece.shape[0], tall)]

    def fetch_rows(source, whole, tail, first):
        return [
            pltpu.make_async_copy(source.at[:, pl.ds(0, width)], whole.at[pl.ds(0, main)], sems.at[first]),
            pltpu.make_async_copy(source.at[:, pl.ds(width, part)], tail, sems.at[first + 1]),
        ]

    def fetch_weights(group, first, wide):
        copies = []
        for n in range(blocks):
            piece, row = pieces[n]
            source = piece.at[pl.ds(row, tall), pl.ds(first, wide)]
            rows = pl.ds(pl.multiple_of(place_of(me_ref[0], n) * tall, tall), tall)
            copies.append(pltpu.make_async_copy(source, w_ref.at[rows, pl.ds(first, wide)], w_sems.at[group, n]))
        return copies

    get_rows = fetch_rows(rows_hbm, x_ref, x_tail, 0)
    get_grads = fetch_rows(grads_hbm, g_ref, g_tail, 2)
    get_in = fetch_weights(0, 0, 2 * hidden)
    get_out = fetch_weights(1, 2 * hidden, hidden)
    for one in get_grads + get_out + get_rows + get_in:
        one.start()

    def unpack(tail, target):
        at = iota((tails, main), 1) - 4 * iota((tails, main), 0)
        for k in range(4):
            pick = jnp.where(at == k, 1.0, 0.0).astype(BF16)
            target[main:, k * part : (k + 1) * part] = dot(pick, tail[...]).astype(BF16)

    def pack(rows, index):
        first = index * (width + part)
        out_ref[:, first : first + width] = rows[:main, :]
        at = iota((main, tails), 0) - 4 * iota((main, tails), 1)
        tail = jnp.zeros((main, part), F32)
        for k in range(4):
            pick = jnp.where(at == k, 1.0, 0.0).astype(BF16)
            tail = tail + dot(pick, rows[main:, k * part : (k + 1) * part])
        out_ref[:, first + width : first + width + part] = tail.astype(BF16)
        columns = pl.ds(first, width + part)
        copy = pltpu.make_async_copy(out_ref.at[:, columns], out_hbm.at[:, columns], out_sems.at[index])
        copy.start()
        return copy

    for one in get_grads:
        one.wait()
    unpack(g_tail, g_ref)
    for one in get_out:
        one.wait()
    back = dot(g_ref[...], w_ref[:, 2 * hidden :])
    for one in get_rows:
        one.wait()
    unpack(x_tail, x_ref)
    for one in get_in:
        one.wait()
    both = dot(x_ref[...], w_ref[:, : 2 * hidden])
    gate, up = both[:, :hidden], both[:, hidden:]
    sig = jax.nn.sigmoid(gate)
    silu = gate * sig
    activated = (silu * up).astype(BF16)
    put_out = pack(dot_nt(activated, w_ref[:, 2 * hidden :]).astype(BF16), 0)
    d_gate = (back * up * sig * (1.0 + gate * (1.0 - sig))).astype(BF16)
    d_up = (back * silu).astype(BF16)
    grad = dot_nt(jnp.concatenate([d_gate, d_up], 1), w_ref[:, : 2 * hidden])
    put_grad = pack(grad.astype(BF16), 1)
    put_out.wait()
    put_grad.wait()


def factor_body(groups, ids_hbm, weight_hbm, factor_hbm, ids_ref, weight_ref, factor_ref, sems):
    fetch = [
        pltpu.make_async_copy(ids_hbm, ids_ref, sems.at[0]),
        pltpu.make_async_copy(weight_hbm, weight_ref, sems.at[1]),
    ]
    copy_all(fetch)
    tokens = ids_ref.shape[1]
    rows = groups * BLOCK
    group = iota((groups, tokens), 0)
    factor = jnp.zeros((groups, tokens), F32)
    for route in range(ids_ref.shape[0]):
        here = ids_ref[route : route + 1, :] == group
        factor = factor + jnp.where(here, weight_ref[route : route + 1, :], 0.0)
    spread = jnp.where(iota((rows, groups), 0) // BLOCK == iota((rows, groups), 1), 1.0, 0.0).astype(BF16)
    coarse = factor.astype(BF16)
    fine = (factor - coarse.astype(F32)).astype(BF16)
    keys = slot_keys(ids_ref[...], groups).T
    coarse, fine = dot(spread, coarse).T, dot(spread, fine).T
    place = iota((tokens, rows), 1)
    late = keys == (BLOCK + (place % BLOCK) // 4).astype(F32)
    masks = [keys == (place % BLOCK).astype(F32)] + [late & (place % 4 == k) for k in range(4)]
    for n, mask in enumerate(masks):
        factor_ref[:, 2 * n * rows : (2 * n + 1) * rows] = jnp.where(mask, coarse, 0.0).astype(BF16)
        factor_ref[:, (2 * n + 1) * rows : (2 * n + 2) * rows] = jnp.where(mask, fine, 0.0).astype(BF16)
    copy_all([pltpu.make_async_copy(factor_ref, factor_hbm, sems.at[2])])


def tables_body(
    groups, me_ref, len_hbm, parent_hbm, ids_hbm, weight_hbm, gate_hbm, up_hbm, down_hbm,
    w_hbm, bias_hbm, factor_hbm,
    len_ref, parent_ref, bias_ref, ids_ref, weight_ref, factor_ref, down_ref, w_ref,
    bias_sems, factor_sems, put_sem, w_sems,
):
    put = bias_body(me_ref, len_hbm, parent_hbm, bias_hbm, len_ref, parent_ref, bias_ref, bias_sems, put_sem)
    factor_body(groups, ids_hbm, weight_hbm, factor_hbm, ids_ref, weight_ref, factor_ref, factor_sems)
    pack_w_body(gate_hbm, up_hbm, down_hbm, w_hbm, down_ref, w_ref, w_sems)
    put.wait()


def combine_body(
    back_hbm, stream_hbm, cot_hbm, gain_hbm, factor_hbm, mixed_hbm, grad_hbm,
    back_ref, stream_ref, cot_ref, gain_ref, factor_ref, mixed_ref, moe_ref, sum_ref, sems, in_sems,
):
    packed = back_hbm.shape[1] // 2
    halves = [
        pltpu.make_async_copy(
            back_hbm.at[:, pl.ds(i * packed, packed)], back_ref.at[:, pl.ds(i * packed, packed)], sems.at[i]
        )
        for i in range(2)
    ]
    others = [
        pltpu.make_async_copy(source, target, in_sems.at[n])
        for n, (source, target) in enumerate(
            ((factor_hbm, factor_ref), (stream_hbm, stream_ref), (cot_hbm, cot_ref), (gain_hbm, gain_ref))
        )
    ]
    for one in others[:1] + halves[:1] + others[1:] + halves[1:]:
        one.start()
    width = stream_hbm.shape[1]
    part = width // 4
    rows = back_hbm.shape[0]
    others[0].wait()

    def weighted(n, rows_back):
        a = factor_ref[:, 2 * n * rows : (2 * n + 1) * rows]
        b = factor_ref[:, (2 * n + 1) * rows : (2 * n + 2) * rows]
        return dot(a, rows_back) + dot(b, rows_back)

    def gather(index, target):
        halves[index].wait()
        first = index * packed
        target[...] = weighted(0, back_ref[:, first : first + width])
        tail = back_ref[:, first + width : first + packed]
        for k in range(4):
            target[:, k * part : (k + 1) * part] += weighted(1 + k, tail)

    gather(0, moe_ref)
    for one in others[1:]:
        one.wait()
    stream = stream_ref[...]
    mixed_ref[...] = (stream + moe_ref[...]).astype(BF16)
    put_mixed = pltpu.make_async_copy(mixed_ref, mixed_hbm, sems.at[4])
    put_mixed.start()
    gather(1, sum_ref)
    scale_back = lax.rsqrt(jnp.mean(stream * stream, -1, keepdims=True) + 1e-06)
    gain_grad = gain_ref[...] * sum_ref[...]
    inner = jnp.mean(stream * gain_grad, -1, keepdims=True)
    moe_ref[...] = cot_ref[...].astype(F32) + scale_back * gain_grad - stream * (scale_back**3 * inner)
    put_grad = pltpu.make_async_copy(moe_ref, grad_hbm, sems.at[5])
    put_grad.start()
    put_mixed.wait()
    put_grad.wait()


def on_device(
    queries,
    key_rows,
    values,
    residual,
    seg_lengths,
    seg_parent,
    ln_gain,
    w_gate,
    w_up,
    w_down,
    expert_ids,
    gate_weights,
    cotangent,
):
    groups = lax.axis_size("exp")
    members = lax.axis_size("ctx")
    tokens, width = residual.shape[1], residual.shape[2]
    kv_width = key_rows.shape[2] + values.shape[2]
    hidden = w_gate.shape[2]
    slab = members * tokens
    rows = groups * BLOCK
    packed = width + width // 4
    shape = jax.ShapeDtypeStruct
    me = lax.axis_index("ctx").astype(jnp.int32).reshape(1)
    ids_t = expert_ids[0].T
    gain = ln_gain.reshape(1, width)

    in_smem = pl.BlockSpec(memory_space=pltpu.SMEM)
    anywhere = pl.BlockSpec(memory_space=pl.ANY)
    in_hbm = pl.BlockSpec(memory_space=pltpu.HBM)
    copy_sem = pltpu.SemaphoreType.DMA

    kv = call(
        pack_kv_body,
        shape((tokens, kv_width), BF16),
        [pltpu.VMEM((tokens, kv_width), BF16), copy_sem((3,))],
        [in_hbm] * 2,
        in_hbm,
    )(key_rows[0], values[0])
    def send(rows_out, target):
        return lax.ppermute(rows_out, "ctx", [(i, target(i)) for i in range(members)])

    def along_x(i, step):
        return (i // 4 + step) % 4 * 4 + i % 4

    def cross(rows_out):
        return send(rows_out, lambda i: i ^ 1)

    def stack(pieces, after=(), flops=0):
        height = sum(piece.shape[0] for piece in pieces)
        return call(
            functools.partial(stack_body, len(pieces)),
            shape((height, pieces[0].shape[1]), BF16),
            [copy_sem((len(pieces),))],
            [in_hbm] * len(pieces) + [anywhere] * len(after),
            in_hbm,
            flops=flops,
            moved=1 << 20,
            vmem=ROOMY,
        )(*pieces, *after)

    w_own, bias, factors = call(
        functools.partial(tables_body, groups),
        (shape((tokens, 3 * hidden), BF16), shape((tokens, slab), F32), shape((tokens, 10 * rows), BF16)),
        [
            pltpu.VMEM(seg_lengths.shape, jnp.int32),
            pltpu.VMEM(seg_parent.shape, jnp.int32),
            pltpu.VMEM((tokens, slab), F32),
            pltpu.VMEM(ids_t.shape, jnp.int32),
            pltpu.VMEM(ids_t.shape, F32),
            pltpu.VMEM((tokens, 10 * rows), BF16),
            pltpu.VMEM(w_down.shape[1:], BF16),
            pltpu.VMEM((tokens, 3 * hidden), BF16),
            copy_sem((2,)),
            copy_sem((3,)),
            copy_sem((1,)),
            copy_sem((4,)),
        ],
        [in_smem] + [in_hbm] * 7,
        (in_hbm, in_hbm, in_hbm),
        moved=2 << 20,
    )(me, seg_lengths, seg_parent, ids_t, gate_weights[0].T, w_gate[0], w_up[0], w_down[0])
    send_grad = call(
        functools.partial(scatter_body, groups),
        shape((rows, packed), BF16),
        [
            pltpu.VMEM((tokens, width), BF16),
            pltpu.VMEM(ids_t.shape, jnp.int32),
            pltpu.VMEM((rows, packed), BF16),
            copy_sem((3,)),
        ],
        [in_hbm] * 2,
        in_hbm,
        flops=2 * rows * tokens * width,
        moved=2 << 20,
    )(cotangent[0], ids_t)

    w_pair = send(w_own, lambda i: i ^ 2)
    kv_both = stack([kv, send(kv, lambda i: i ^ 2)])
    kv_near, kv_far, kv_last = (send(kv_both, functools.partial(along_x, step=step)) for step in (1, 2, 3))
    kv_mine = stack([kv_both, kv_near, kv_far, kv_last], [w_own])
    kv_core = cross(kv_mine)

    def exchange(sent):
        return lax.all_to_all(
            sent.reshape(groups, BLOCK, sent.shape[1]), "exp", split_axis=0, concat_axis=0, tiled=True
        ).reshape(sent.shape)

    arrived_grad = exchange(send_grad)
    stream, send_input = call(
        functools.partial(attend_body, groups),
        (shape((tokens, width), F32), shape((rows, packed), BF16)),
        [
            pltpu.VMEM((tokens, width), BF16),
            pltpu.VMEM((slab, kv_width), BF16),
            pltpu.VMEM((tokens, width), BF16),
            pltpu.VMEM((tokens, slab), F32),
            pltpu.VMEM((1, width), F32),
            pltpu.VMEM(ids_t.shape, jnp.int32),
            pltpu.VMEM((tokens, width), F32),
            pltpu.VMEM((rows, packed), BF16),
            copy_sem((9,)),
        ],
        [in_hbm] * 7,
        (in_hbm, in_hbm),
        vmem=62 << 20,
        flops=24 * tokens * slab * width,
        moved=8 << 20,
    )(queries[0], kv_mine, kv_core, residual[0], bias, gain, ids_t)
    arrived_in = exchange(send_input)
    w_both = stack([w_own, w_pair], [send_input], 16 << 30)
    w_near = send(w_both, functools.partial(along_x, step=1))
    w_last = send(w_both, functools.partial(along_x, step=3))
    w_far_own = send(w_near[:tokens], functools.partial(along_x, step=1))
    w_far_pair = send(w_last[tokens:], functools.partial(along_x, step=3))
    w_pieces = [w_both, w_near, w_far_own, w_far_pair, w_last]
    w_pieces = w_pieces + [cross(piece) for piece in w_pieces]
    returned = call(
        expert_body,
        shape((rows, 2 * packed), BF16),
        [
            pltpu.VMEM((groups * CAP, width), BF16),
            pltpu.VMEM((rows, packed - width), BF16),
            pltpu.VMEM((groups * CAP, width), BF16),
            pltpu.VMEM((rows, packed - width), BF16),
            pltpu.VMEM((width, 3 * hidden), BF16),
            pltpu.VMEM((rows, 2 * packed), BF16),
            copy_sem((4,)),
            copy_sem((2, members)),
            copy_sem((2,)),
        ],
        [in_smem] + [in_hbm] * (2 + len(w_pieces)),
        in_hbm,
        flops=12 * groups * CAP * width * hidden,
        moved=10 << 20,
    )(me, arrived_in, arrived_grad, *w_pieces)
    back = exchange(returned)
    mixed_out, stream_grad = call(
        combine_body,
        (shape((tokens, width), BF16), shape((tokens, width), F32)),
        [
            pltpu.VMEM((rows, 2 * packed), BF16),
            pltpu.VMEM((tokens, width), F32),
            pltpu.VMEM((tokens, width), BF16),
            pltpu.VMEM((1, width), F32),
            pltpu.VMEM((tokens, 10 * rows), BF16),
            pltpu.VMEM((tokens, width), BF16),
            pltpu.VMEM((tokens, width), F32),
            pltpu.VMEM((tokens, width), F32),
            copy_sem((6,)),
            copy_sem((4,)),
        ],
        [in_hbm] * 5,
        (in_hbm, in_hbm),
    )(back, stream, cotangent[0], gain, factors)
    return (mixed_out[None], stream_grad[None])


def solution(mesh):
    placed = (
        P("exp", "ctx", None),
        P("exp", "ctx", None),
        P("exp", "ctx", None),
        P("exp", "ctx", None),
        P("exp", None),
        P("exp", None),
        P(),
        P("exp", "ctx", None),
        P("exp", "ctx", None),
        P("exp", None, "ctx"),
        P("exp", "ctx", None),
        P("exp", "ctx", None),
        P("exp", "ctx", None),
    )
    return jax.shard_map(
        on_device,
        mesh=mesh,
        in_specs=placed,
        out_specs=(P("exp", "ctx", None), P("exp", "ctx", None)),
        check_vma=False,
    )
```

```python
import functools
import math

import jax
import jax.numpy as jnp
from jax import lax
from jax.experimental import pallas as pl
from jax.experimental.pallas import tpu as pltpu
from jax.sharding import PartitionSpec as P

HEAD_DIM = 128
TOPK = 8
CAP = 10
BLOCK = 8
NO_SLOT = 512.0
TOGETHER = 8
ROOMY = 28 << 20
ALONE = 60 << 20
HIDDEN = -1e30
F32 = jnp.float32
BF16 = jnp.bfloat16
NT = (((1,), (1,)), ((), ()))


def iota(shape, dim):
    return lax.broadcasted_iota(jnp.int32, shape, dim)


def dot(a, b):
    return jnp.dot(a, b, preferred_element_type=F32)


def dot_nt(a, b):
    return lax.dot_general(a, b, NT, preferred_element_type=F32)


def call(body, outs, scratch=(), in_specs=None, out_specs=None, flops=0, moved=0, vmem=ALONE):
    specs = {} if in_specs is None else {"in_specs": in_specs, "out_specs": out_specs}
    return pl.pallas_call(
        body,
        out_shape=outs,
        **specs,
        scratch_shapes=list(scratch),
        compiler_params=pltpu.CompilerParams(vmem_limit_bytes=vmem),
        cost_estimate=pl.CostEstimate(flops=flops, bytes_accessed=moved, transcendentals=0),
    )


def slot_keys(ids_t, groups):
    tokens = ids_t.shape[1]
    group = iota((groups, tokens), 0)
    named = jnp.zeros((groups, tokens), F32)
    for route in range(ids_t.shape[0]):
        named = named + jnp.where(ids_t[route : route + 1, :] == group, 1.0, 0.0)
    before = (iota((tokens, tokens), 0) < iota((tokens, tokens), 1)).astype(F32)
    rank = dot(named.astype(BF16), before.astype(BF16))
    key = jnp.where(named > 0.5, rank, NO_SLOT).astype(BF16)
    rows = groups * BLOCK
    spread = (iota((rows, groups), 0) // BLOCK == iota((rows, groups), 1)).astype(F32)
    return dot(spread.astype(BF16), key)


def dispatch(rows, keys, out_ref, out_hbm, sems):
    place = iota(keys.shape, 0)
    width = rows.shape[1]
    part = width // 4
    columns = pl.ds(0, width), pl.ds(width, part)
    copies = [pltpu.make_async_copy(out_ref.at[:, c], out_hbm.at[:, c], sems.at[n]) for n, c in enumerate(columns)]
    pick = jnp.where(keys == (place % BLOCK).astype(F32), 1.0, 0.0).astype(BF16)
    out_ref[:, :width] = dot(pick, rows).astype(BF16)
    copies[0].start()
    late = keys == (BLOCK + (place % BLOCK) // 4).astype(F32)
    tail = jnp.zeros((keys.shape[0], part), F32)
    for k in range(4):
        pick = jnp.where(late & (place % 4 == k), 1.0, 0.0).astype(BF16)
        tail = tail + dot(pick, rows[:, k * part : (k + 1) * part])
    out_ref[:, width:] = tail.astype(BF16)
    copies[1].start()
    return copies


def copy_all(copies):
    for one in copies:
        one.start()
    for one in copies:
        one.wait()


def pack_kv_body(key_hbm, value_hbm, kv_hbm, kv_ref, sems):
    half = key_hbm.shape[1]
    copy_all(
        [
            pltpu.make_async_copy(key_hbm, kv_ref.at[:, pl.ds(0, half)], sems.at[0]),
            pltpu.make_async_copy(value_hbm, kv_ref.at[:, pl.ds(half, half)], sems.at[1]),
        ]
    )
    copy_all([pltpu.make_async_copy(kv_ref, kv_hbm, sems.at[2])])


def pack_w_body(gate_hbm, up_hbm, down_hbm, w_hbm, down_ref, w_ref, sems):
    hidden = gate_hbm.shape[1]
    copies = [
        pltpu.make_async_copy(down_hbm, down_ref, sems.at[0]),
        pltpu.make_async_copy(gate_hbm, w_ref.at[:, pl.ds(0, hidden)], sems.at[1]),
        pltpu.make_async_copy(up_hbm, w_ref.at[:, pl.ds(hidden, hidden)], sems.at[2]),
    ]
    copy_all(copies)
    w_ref[:, 2 * hidden :] = down_ref[...].T
    copy_all([pltpu.make_async_copy(w_ref, w_hbm, sems.at[3])])


def place_of(me, n):
    x, y, core = me // 4, (me // 2) % 2, me % 2
    return (x + 4 - n % 8 // 2) % 4 * 4 + (y + n) % 2 * 2 + (core + n // 8) % 2


def stack_body(count, *refs):
    out_ref, sems = refs[-2:]
    first, copies = 0, []
    for n, piece in enumerate(refs[:count]):
        copies.append(pltpu.make_async_copy(piece, out_ref.at[pl.ds(first, piece.shape[0])], sems.at[n]))
        first += piece.shape[0]
    copy_all(copies)


def scatter_body(groups, rows_hbm, ids_hbm, send_hbm, rows_ref, ids_ref, send_ref, sems, out_sems):
    get_ids = pltpu.make_async_copy(ids_hbm, ids_ref, sems.at[0])
    get_rows = pltpu.make_async_copy(rows_hbm, rows_ref, sems.at[1])
    get_ids.start()
    get_rows.start()
    get_ids.wait()
    keys = slot_keys(ids_ref[...], groups)
    get_rows.wait()
    for one in dispatch(rows_ref[...], keys, send_ref, send_hbm, out_sems):
        one.wait()


def bias_body(me_ref, len_hbm, parent_hbm, bias_hbm, len_ref, parent_ref, bias_ref, sems, put_sem):
    copy_all(
        [
            pltpu.make_async_copy(len_hbm, len_ref, sems.at[0]),
            pltpu.make_async_copy(parent_hbm, parent_ref, sems.at[1]),
        ]
    )
    segs = len_ref.shape[1]
    rows = bias_ref.shape[0]
    low, high = iota((segs, segs), 0), iota((segs, segs), 1)
    len_row = len_ref[...].astype(F32)
    len_col = jnp.sum(jnp.where(low == high, len_row, 0.0), 1, keepdims=True)
    parent_col = jnp.sum(jnp.where(low == high, parent_ref[...].astype(F32), 0.0), 1, keepdims=True)
    start_col = jnp.sum(jnp.where(high < low, len_row, 0.0), 1, keepdims=True)
    start_row = jnp.sum(jnp.where(low < high, len_col, 0.0), 0, keepdims=True)
    finish_col = start_col + len_col
    finish_row = start_row + len_row
    reached = jnp.where((parent_col == high.astype(F32)) | (low == high), 1.0, 0.0)
    for sweep in range(max(1, (segs - 1).bit_length())):
        low_bits = reached.astype(BF16)
        reached = jnp.minimum(dot(low_bits, low_bits), 1.0)
    me = me_ref[0]
    query_pos = (me * rows + iota((rows, 1), 0)).astype(F32)
    member = jnp.where((query_pos >= start_row) & (query_pos < finish_row), 1.0, 0.0)
    query_reach = dot(member.astype(BF16), reached.astype(BF16)).astype(BF16)
    for n in range(bias_ref.shape[1] // rows):
        key_pos = (place_of(me, n) * rows + iota((1, rows), 1)).astype(F32)
        holds = jnp.where((key_pos >= start_col) & (key_pos < finish_col), 1.0, 0.0)
        linked = dot(query_reach, holds.astype(BF16))
        visible = (linked > 0.5) & (key_pos <= query_pos)
        bias_ref[:, n * rows : (n + 1) * rows] = jnp.where(visible, 0.0, HIDDEN)
    put = pltpu.make_async_copy(bias_ref, bias_hbm, put_sem.at[0])
    put.start()
    return put


def attend_body(
    groups,
    q_hbm,
    mine_hbm,
    core_hbm,
    residual_hbm,
    bias_hbm,
    gain_hbm,
    ids_hbm,
    stream_hbm,
    send_hbm,
    q_ref,
    kv_ref,
    residual_ref,
    bias_ref,
    gain_ref,
    ids_ref,
    stream_ref,
    send_ref,
    sems,
    out_sems,
):
    pieces, first, fetch = (mine_hbm, core_hbm), 0, []
    for n, piece in enumerate(pieces):
        fetch.append(pltpu.make_async_copy(piece, kv_ref.at[pl.ds(first, piece.shape[0])], sems.at[n]))
        first += piece.shape[0]
    fetch += [
        pltpu.make_async_copy(q_hbm, q_ref, sems.at[2]),
        pltpu.make_async_copy(bias_hbm, bias_ref, sems.at[3]),
        pltpu.make_async_copy(residual_hbm, residual_ref, sems.at[6]),
        pltpu.make_async_copy(gain_hbm, gain_ref, sems.at[7]),
        pltpu.make_async_copy(ids_hbm, ids_ref, sems.at[8]),
    ]
    for one in fetch:
        one.start()
    for one in fetch[:4]:
        one.wait()
    kv_heads = kv_ref.shape[1] // (2 * HEAD_DIM)
    per_kv = q_ref.shape[1] // HEAD_DIM // kv_heads
    factor = HEAD_DIM**-0.5 * math.log2(math.e)
    for g in range(kv_heads):
        keys = kv_ref[:, g * HEAD_DIM : (g + 1) * HEAD_DIM]
        vals = kv_ref[:, (kv_heads + g) * HEAD_DIM : (kv_heads + g + 1) * HEAD_DIM]

        def heads(i, carry):
            at = [pl.multiple_of((g * per_kv + i * TOGETHER + j) * HEAD_DIM, HEAD_DIM) for j in range(TOGETHER)]
            scores = [dot_nt(q_ref[:, pl.ds(a, HEAD_DIM)], keys) + bias_ref[...] for a in at]
            for a, score in zip(at, scores):
                top = jnp.max(score, -1, keepdims=True)
                probs = jnp.exp2((score - top) * factor)
                denom = jnp.sum(probs, -1, keepdims=True)
                attended = (dot(probs.astype(BF16), vals) / denom).astype(BF16)
                stream_ref[:, pl.ds(a, HEAD_DIM)] = attended.astype(F32)
            return carry

        lax.fori_loop(0, per_kv // TOGETHER, heads, 0)
    for one in fetch[4:]:
        one.wait()
    stream = residual_ref[...].astype(F32) + stream_ref[...]
    stream_ref[...] = stream
    keep = pltpu.make_async_copy(stream_ref, stream_hbm, sems.at[4])
    keep.start()
    scale_back = lax.rsqrt(jnp.mean(stream * stream, -1, keepdims=True) + 1e-06)
    normed = (stream * scale_back * gain_ref[...]).astype(BF16)
    for one in dispatch(normed, slot_keys(ids_ref[...], groups), send_ref, send_hbm, out_sems) + [keep]:
        one.wait()


def expert_body(me_ref, rows_hbm, grads_hbm, *refs):
    out_hbm, x_ref, x_tail, g_ref, g_tail, w_ref, out_ref, sems, w_sems, out_sems = refs[-10:]
    width = w_ref.shape[0]
    hidden = w_ref.shape[1] // 3
    main = rows_hbm.shape[0]
    part = width // 4
    tails = main // 4
    blocks = w_sems.shape[1]
    tall = width // blocks
    pieces = [(piece, row) for piece in refs[:-10] for row in range(0, piece.shape[0], tall)]

    def fetch_rows(source, whole, tail, first):
        return [
            pltpu.make_async_copy(source.at[:, pl.ds(0, width)], whole.at[pl.ds(0, main)], sems.at[first]),
            pltpu.make_async_copy(source.at[:, pl.ds(width, part)], tail, sems.at[first + 1]),
        ]

    def fetch_weights(group, first, wide):
        copies = []
        for n in range(blocks):
            piece, row = pieces[n]
            source = piece.at[pl.ds(row, tall), pl.ds(first, wide)]
            rows = pl.ds(pl.multiple_of(place_of(me_ref[0], n) * tall, tall), tall)
            copies.append(pltpu.make_async_copy(source, w_ref.at[rows, pl.ds(first, wide)], w_sems.at[group, n]))
        return copies

    get_rows = fetch_rows(rows_hbm, x_ref, x_tail, 0)
    get_grads = fetch_rows(grads_hbm, g_ref, g_tail, 2)
    get_in = fetch_weights(0, 0, 2 * hidden)
    get_out = fetch_weights(1, 2 * hidden, hidden)
    for one in get_grads + get_out + get_rows + get_in:
        one.start()

    def unpack(tail, target):
        at = iota((tails, main), 1) - 4 * iota((tails, main), 0)
        for k in range(4):
            pick = jnp.where(at == k, 1.0, 0.0).astype(BF16)
            target[main:, k * part : (k + 1) * part] = dot(pick, tail[...]).astype(BF16)

    def pack(rows, index):
        first = index * (width + part)
        out_ref[:, first : first + width] = rows[:main, :]
        at = iota((main, tails), 0) - 4 * iota((main, tails), 1)
        tail = jnp.zeros((main, part), F32)
        for k in range(4):
            pick = jnp.where(at == k, 1.0, 0.0).astype(BF16)
            tail = tail + dot(pick, rows[main:, k * part : (k + 1) * part])
        out_ref[:, first + width : first + width + part] = tail.astype(BF16)
        columns = pl.ds(first, width + part)
        copy = pltpu.make_async_copy(out_ref.at[:, columns], out_hbm.at[:, columns], out_sems.at[index])
        copy.start()
        return copy

    for one in get_grads:
        one.wait()
    unpack(g_tail, g_ref)
    for one in get_out:
        one.wait()
    back = dot(g_ref[...], w_ref[:, 2 * hidden :])
    for one in get_rows:
        one.wait()
    unpack(x_tail, x_ref)
    for one in get_in:
        one.wait()
    both = dot(x_ref[...], w_ref[:, : 2 * hidden])
    gate, up = both[:, :hidden], both[:, hidden:]
    sig = jax.nn.sigmoid(gate)
    silu = gate * sig
    activated = (silu * up).astype(BF16)
    put_out = pack(dot_nt(activated, w_ref[:, 2 * hidden :]).astype(BF16), 0)
    d_gate = (back * up * sig * (1.0 + gate * (1.0 - sig))).astype(BF16)
    d_up = (back * silu).astype(BF16)
    grad = dot_nt(jnp.concatenate([d_gate, d_up], 1), w_ref[:, : 2 * hidden])
    put_grad = pack(grad.astype(BF16), 1)
    put_out.wait()
    put_grad.wait()


def factor_body(groups, ids_hbm, weight_hbm, factor_hbm, ids_ref, weight_ref, factor_ref, sems):
    fetch = [
        pltpu.make_async_copy(ids_hbm, ids_ref, sems.at[0]),
        pltpu.make_async_copy(weight_hbm, weight_ref, sems.at[1]),
    ]
    copy_all(fetch)
    tokens = ids_ref.shape[1]
    rows = groups * BLOCK
    group = iota((groups, tokens), 0)
    factor = jnp.zeros((groups, tokens), F32)
    for route in range(ids_ref.shape[0]):
        here = ids_ref[route : route + 1, :] == group
        factor = factor + jnp.where(here, weight_ref[route : route + 1, :], 0.0)
    spread = jnp.where(iota((rows, groups), 0) // BLOCK == iota((rows, groups), 1), 1.0, 0.0).astype(BF16)
    coarse = factor.astype(BF16)
    fine = (factor - coarse.astype(F32)).astype(BF16)
    keys = slot_keys(ids_ref[...], groups).T
    coarse, fine = dot(spread, coarse).T, dot(spread, fine).T
    place = iota((tokens, rows), 1)
    late = keys == (BLOCK + (place % BLOCK) // 4).astype(F32)
    masks = [keys == (place % BLOCK).astype(F32)] + [late & (place % 4 == k) for k in range(4)]
    for n, mask in enumerate(masks):
        factor_ref[:, 2 * n * rows : (2 * n + 1) * rows] = jnp.where(mask, coarse, 0.0).astype(BF16)
        factor_ref[:, (2 * n + 1) * rows : (2 * n + 2) * rows] = jnp.where(mask, fine, 0.0).astype(BF16)
    copy_all([pltpu.make_async_copy(factor_ref, factor_hbm, sems.at[2])])


def tables_body(
    groups, me_ref, len_hbm, parent_hbm, ids_hbm, weight_hbm, gate_hbm, up_hbm, down_hbm,
    w_hbm, bias_hbm, factor_hbm,
    len_ref, parent_ref, bias_ref, ids_ref, weight_ref, factor_ref, down_ref, w_ref,
    bias_sems, factor_sems, put_sem, w_sems,
):
    put = bias_body(me_ref, len_hbm, parent_hbm, bias_hbm, len_ref, parent_ref, bias_ref, bias_sems, put_sem)
    factor_body(groups, ids_hbm, weight_hbm, factor_hbm, ids_ref, weight_ref, factor_ref, factor_sems)
    pack_w_body(gate_hbm, up_hbm, down_hbm, w_hbm, down_ref, w_ref, w_sems)
    put.wait()


def combine_body(
    back_hbm, stream_hbm, cot_hbm, gain_hbm, factor_hbm, mixed_hbm, grad_hbm,
    back_ref, stream_ref, cot_ref, gain_ref, factor_ref, mixed_ref, moe_ref, sum_ref, sems, in_sems,
):
    packed = back_hbm.shape[1] // 2
    halves = [
        pltpu.make_async_copy(
            back_hbm.at[:, pl.ds(i * packed, packed)], back_ref.at[:, pl.ds(i * packed, packed)], sems.at[i]
        )
        for i in range(2)
    ]
    others = [
        pltpu.make_async_copy(source, target, in_sems.at[n])
        for n, (source, target) in enumerate(
            ((factor_hbm, factor_ref), (stream_hbm, stream_ref), (cot_hbm, cot_ref), (gain_hbm, gain_ref))
        )
    ]
    for one in others[:1] + halves[:1] + others[1:] + halves[1:]:
        one.start()
    width = stream_hbm.shape[1]
    part = width // 4
    rows = back_hbm.shape[0]
    others[0].wait()

    def weighted(n, rows_back):
        a = factor_ref[:, 2 * n * rows : (2 * n + 1) * rows]
        b = factor_ref[:, (2 * n + 1) * rows : (2 * n + 2) * rows]
        return dot(a, rows_back) + dot(b, rows_back)

    def gather(index, target):
        halves[index].wait()
        first = index * packed
        target[...] = weighted(0, back_ref[:, first : first + width])
        tail = back_ref[:, first + width : first + packed]
        for k in range(4):
            target[:, k * part : (k + 1) * part] += weighted(1 + k, tail)

    gather(0, moe_ref)
    for one in others[1:]:
        one.wait()
    stream = stream_ref[...]
    mixed_ref[...] = (stream + moe_ref[...]).astype(BF16)
    put_mixed = pltpu.make_async_copy(mixed_ref, mixed_hbm, sems.at[4])
    put_mixed.start()
    gather(1, sum_ref)
    scale_back = lax.rsqrt(jnp.mean(stream * stream, -1, keepdims=True) + 1e-06)
    gain_grad = gain_ref[...] * sum_ref[...]
    inner = jnp.mean(stream * gain_grad, -1, keepdims=True)
    moe_ref[...] = cot_ref[...].astype(F32) + scale_back * gain_grad - stream * (scale_back**3 * inner)
    put_grad = pltpu.make_async_copy(moe_ref, grad_hbm, sems.at[5])
    put_grad.start()
    put_mixed.wait()
    put_grad.wait()


def on_device(
    queries,
    key_rows,
    values,
    residual,
    seg_lengths,
    seg_parent,
    ln_gain,
    w_gate,
    w_up,
    w_down,
    expert_ids,
    gate_weights,
    cotangent,
):
    groups = lax.axis_size("exp")
    members = lax.axis_size("ctx")
    tokens, width = residual.shape[1], residual.shape[2]
    kv_width = key_rows.shape[2] + values.shape[2]
    hidden = w_gate.shape[2]
    slab = members * tokens
    rows = groups * BLOCK
    packed = width + width // 4
    shape = jax.ShapeDtypeStruct
    me = lax.axis_index("ctx").astype(jnp.int32).reshape(1)
    ids_t = expert_ids[0].T
    gain = ln_gain.reshape(1, width)

    in_smem = pl.BlockSpec(memory_space=pltpu.SMEM)
    anywhere = pl.BlockSpec(memory_space=pl.ANY)
    in_hbm = pl.BlockSpec(memory_space=pltpu.HBM)
    copy_sem = pltpu.SemaphoreType.DMA

    kv = call(
        pack_kv_body,
        shape((tokens, kv_width), BF16),
        [pltpu.VMEM((tokens, kv_width), BF16), copy_sem((3,))],
        [in_hbm] * 2,
        in_hbm,
    )(key_rows[0], values[0])
    def send(rows_out, target):
        return lax.ppermute(rows_out, "ctx", [(i, target(i)) for i in range(members)])

    def along_x(i, step):
        return (i // 4 + step) % 4 * 4 + i % 4

    def cross(rows_out):
        return send(rows_out, lambda i: i ^ 1)

    def stack(pieces, after=(), flops=0):
        height = sum(piece.shape[0] for piece in pieces)
        return call(
            functools.partial(stack_body, len(pieces)),
            shape((height, pieces[0].shape[1]), BF16),
            [copy_sem((len(pieces),))],
            [in_hbm] * len(pieces) + [anywhere] * len(after),
            in_hbm,
            flops=flops,
            moved=1 << 20,
            vmem=ROOMY,
        )(*pieces, *after)

    w_own, bias, factors = call(
        functools.partial(tables_body, groups),
        (shape((tokens, 3 * hidden), BF16), shape((tokens, slab), F32), shape((tokens, 10 * rows), BF16)),
        [
            pltpu.VMEM(seg_lengths.shape, jnp.int32),
            pltpu.VMEM(seg_parent.shape, jnp.int32),
            pltpu.VMEM((tokens, slab), F32),
            pltpu.VMEM(ids_t.shape, jnp.int32),
            pltpu.VMEM(ids_t.shape, F32),
            pltpu.VMEM((tokens, 10 * rows), BF16),
            pltpu.VMEM(w_down.shape[1:], BF16),
            pltpu.VMEM((tokens, 3 * hidden), BF16),
            copy_sem((2,)),
            copy_sem((3,)),
            copy_sem((1,)),
            copy_sem((4,)),
        ],
        [in_smem] + [in_hbm] * 7,
        (in_hbm, in_hbm, in_hbm),
        moved=2 << 20,
    )(me, seg_lengths, seg_parent, ids_t, gate_weights[0].T, w_gate[0], w_up[0], w_down[0])
    send_grad = call(
        functools.partial(scatter_body, groups),
        shape((rows, packed), BF16),
        [
            pltpu.VMEM((tokens, width), BF16),
            pltpu.VMEM(ids_t.shape, jnp.int32),
            pltpu.VMEM((rows, packed), BF16),
            copy_sem((2,)),
            copy_sem((2,)),
        ],
        [in_hbm] * 2,
        in_hbm,
        flops=2 * rows * tokens * width,
        moved=2 << 20,
    )(cotangent[0], ids_t)

    w_pair = send(w_own, lambda i: i ^ 2)
    kv_both = stack([kv, send(kv, lambda i: i ^ 2)])
    kv_near, kv_far, kv_last = (send(kv_both, functools.partial(along_x, step=step)) for step in (1, 2, 3))
    kv_mine = stack([kv_both, kv_near, kv_far, kv_last], [w_own])
    kv_core = cross(kv_mine)

    def exchange(sent):
        return lax.all_to_all(
            sent.reshape(groups, BLOCK, sent.shape[1]), "exp", split_axis=0, concat_axis=0, tiled=True
        ).reshape(sent.shape)

    arrived_grad = exchange(send_grad)
    stream, send_input = call(
        functools.partial(attend_body, groups),
        (shape((tokens, width), F32), shape((rows, packed), BF16)),
        [
            pltpu.VMEM((tokens, width), BF16),
            pltpu.VMEM((slab, kv_width), BF16),
            pltpu.VMEM((tokens, width), BF16),
            pltpu.VMEM((tokens, slab), F32),
            pltpu.VMEM((1, width), F32),
            pltpu.VMEM(ids_t.shape, jnp.int32),
            pltpu.VMEM((tokens, width), F32),
            pltpu.VMEM((rows, packed), BF16),
            copy_sem((9,)),
            copy_sem((2,)),
        ],
        [in_hbm] * 7,
        (in_hbm, in_hbm),
        vmem=62 << 20,
        flops=24 * tokens * slab * width,
        moved=8 << 20,
    )(queries[0], kv_mine, kv_core, residual[0], bias, gain, ids_t)
    arrived_in = exchange(send_input)
    w_both = stack([w_own, w_pair], [send_input], 16 << 30)
    w_near = send(w_both, functools.partial(along_x, step=1))
    w_last = send(w_both, functools.partial(along_x, step=3))
    w_far_own = send(w_near[:tokens], functools.partial(along_x, step=1))
    w_far_pair = send(w_last[tokens:], functools.partial(along_x, step=3))
    w_pieces = [w_both, w_near, w_far_own, w_far_pair, w_last]
    w_pieces = w_pieces + [cross(piece) for piece in w_pieces]
    returned = call(
        expert_body,
        shape((rows, 2 * packed), BF16),
        [
            pltpu.VMEM((groups * CAP, width), BF16),
            pltpu.VMEM((rows, packed - width), BF16),
            pltpu.VMEM((groups * CAP, width), BF16),
            pltpu.VMEM((rows, packed - width), BF16),
            pltpu.VMEM((width, 3 * hidden), BF16),
            pltpu.VMEM((rows, 2 * packed), BF16),
            copy_sem((4,)),
            copy_sem((2, members)),
            copy_sem((2,)),
        ],
        [in_smem] + [in_hbm] * (2 + len(w_pieces)),
        in_hbm,
        flops=12 * groups * CAP * width * hidden,
        moved=10 << 20,
    )(me, arrived_in, arrived_grad, *w_pieces)
    back = exchange(returned)
    mixed_out, stream_grad = call(
        combine_body,
        (shape((tokens, width), BF16), shape((tokens, width), F32)),
        [
            pltpu.VMEM((rows, 2 * packed), BF16),
            pltpu.VMEM((tokens, width), F32),
            pltpu.VMEM((tokens, width), BF16),
            pltpu.VMEM((1, width), F32),
            pltpu.VMEM((tokens, 10 * rows), BF16),
            pltpu.VMEM((tokens, width), BF16),
            pltpu.VMEM((tokens, width), F32),
            pltpu.VMEM((tokens, width), F32),
            copy_sem((6,)),
            copy_sem((4,)),
        ],
        [in_hbm] * 5,
        (in_hbm, in_hbm),
    )(back, stream, cotangent[0], gain, factors)
    return (mixed_out[None], stream_grad[None])


def solution(mesh):
    placed = (
        P("exp", "ctx", None),
        P("exp", "ctx", None),
        P("exp", "ctx", None),
        P("exp", "ctx", None),
        P("exp", None),
        P("exp", None),
        P(),
        P("exp", "ctx", None),
        P("exp", "ctx", None),
        P("exp", None, "ctx"),
        P("exp", "ctx", None),
        P("exp", "ctx", None),
        P("exp", "ctx", None),
    )
    return jax.shard_map(
        on_device,
        mesh=mesh,
        in_specs=placed,
        out_specs=(P("exp", "ctx", None), P("exp", "ctx", None)),
        check_vma=False,
    )
```
